32 devices in a mesh: pipe: 4 (over y, x), seq: 8 (over z, core).
Axes of the slice: x: 2, y: 2, z: 4, core: 2. Of those that a mesh axis runs over, the one named last changes fastest.
Arguments:
- queries: bfloat16 [4, 2, 1024, 2048], P('pipe', None, 'seq'), may hold values from -120 to 120
- keys: bfloat16 [4, 2, 1024, 512], P('pipe', None, 'seq'), may hold values from -5 to 5
- values: bfloat16 [4, 2, 1024, 512], P('pipe', None, 'seq'), may hold values from -6 to 6
- out_grad: bfloat16 [2, 1024, 2048], P(None, 'seq'), may hold values from -6 to 6
- segments: int32 [2, 1024], replicated, may hold values from 0 to 15, never falling along the last dimension, each value on 1 to 256 neighbouring positions
Outputs:
- query_grads: bfloat16 [4, 2, 1024, 2048], P('pipe', None, 'seq')
- key_grads: bfloat16 [4, 2, 1024, 512], P('pipe', None, 'seq')
- value_grads: bfloat16 [4, 2, 1024, 512], P('pipe', None, 'seq')
The draws below stay inside these ranges and needn't reach their ends.
Inputs may be any that keep to these rules, and one draw needn't show every extreme that they name: `segments`: segment numbers never fall along a micro-batch.
All inputs are finite; a program needn't handle non-finite values.
Results may differ from the reference program's by a relative error of at most 0.014.
Values may be sent and summed in bfloat16 or wider, within the bound.
A program may use at most 64 MiB of HBM per device.

```python
import math
import jax
import jax.numpy as jnp
import numpy as np
from jax import lax

TOK_DEV = 128
MICRO = 2
HQ = 16
HK = 4
DH = 128
WINDOW = 128
SECTIONS = 4
TOKENS = 1024
N_SEQ = 8


def drawn_pair(key):
    key_base = jnp.clip(jax.random.normal(jax.random.fold_in(key, 11), (SECTIONS, MICRO, TOKENS, HK, DH), jnp.float32), -5.0, 5.0)
    query_base = jnp.clip(jax.random.normal(jax.random.fold_in(key, 12), (SECTIONS, MICRO, TOKENS, HK, HQ // HK, DH), jnp.float32), -5.0, 5.0)
    return (query_base, key_base)


def draw_queries(key, part):
    query_mod, key_mod = drawn_pair(jax.random.fold_in(key, 5))
    return query_mod.reshape(SECTIONS, MICRO, TOKENS, HQ * DH).astype(jnp.bfloat16)


def draw_keys(key, part):
    query_mod, key_mod = drawn_pair(jax.random.fold_in(key, 5))
    return key_mod.reshape(SECTIONS, MICRO, TOKENS, HK * DH).astype(jnp.bfloat16)


def shard_levels(rng, extent, pieces, low, largest):
    def one(axis_at, shards_of):
        draws = jax.random.uniform(jax.random.fold_in(jax.random.fold_in(rng, 6), axis_at), (shards_of,), jnp.float32, low / len(pieces), largest / len(pieces))
        return jnp.repeat(jnp.exp(draws), extent[axis_at] // shards_of).reshape((-1,) + (1,) * (len(extent) - axis_at - 1))

    factor_of = one(*pieces[0])
    for cut in pieces[1:]:
        factor_of = factor_of * one(*cut)
    return factor_of


def length_profile(number_of, total, bound, slope):
    portions = [(1 << 20) // math.isqrt(rank ** slope) + 1 for rank in range(2, number_of + 1)]
    rest, given = total - bound - (number_of - 1), [1] * (number_of - 1)
    while rest > 0:
        movable = [i for i in range(number_of - 1) if given[i] < bound]
        mass, left = sum([portions[i] for i in movable]), rest
        for i in movable:
            addition = min(bound - given[i], max(1, left * portions[i] // mass), rest)
            given[i] = given[i] + addition
            rest = rest - addition
    return np.array([bound] + given)


def ragged_sizes(stream_key, count, total, bound, slope):
    if count == 2:
        one = jax.random.randint(stream_key, (), max(1, total - bound), min(bound, total - 1) + 1)
        return jnp.stack([one, total - one])
    sizes = jnp.asarray(length_profile(count, total, bound, slope), jnp.int32)
    twos = (count - 1) // 2
    donor, sink = sizes[1:1 + 2 * twos:2], sizes[2:2 + 2 * twos:2]
    slack = jnp.minimum(donor - 1, bound - sink)
    passed = jax.random.randint(jax.random.fold_in(stream_key, 1), (twos,), 0, 1 << 20) % (slack + 1)
    sizes = sizes.at[1:1 + 2 * twos:2].set(donor - passed).at[2:2 + 2 * twos:2].set(sink + passed)
    return sizes[jax.random.permutation(jax.random.fold_in(stream_key, 2), count)]


def bell_draw(rng, dims, deviation, limit, cuts=(), kind=jnp.bfloat16):
    loudness = shard_levels(rng, dims, cuts, -0.22, 0.18) if cuts else 1.0
    result = jax.random.normal(rng, dims, jnp.float32) * deviation * loudness
    return jnp.minimum(jnp.maximum(result, -limit), limit).astype(kind)


def setup_inputs(seed: int = 0) -> dict:
    key_of = jax.random.split(jax.random.key(seed), 6)
    queries = draw_queries(jax.random.fold_in(key_of[5], 71), 0)
    keys = draw_keys(jax.random.fold_in(key_of[5], 71), 0)
    values = bell_draw(key_of[2], (SECTIONS, MICRO, TOKENS, HK * DH), 1.0, 6.0, ((0, 4), (2, 8)))
    out_grad = bell_draw(key_of[3], (MICRO, TOKENS, HQ * DH), 1.0, 6.0, ((1, 8),))
    segments = jax.vmap(lambda own: jnp.searchsorted(jnp.cumsum(ragged_sizes(own, 2 * N_SEQ, TOKENS, 2 * TOK_DEV, 2)), jnp.arange(TOKENS), side="right"))(jax.random.split(key_of[4], MICRO)).reshape((MICRO, TOKENS)).astype(jnp.int32)
    return dict(queries=queries, keys=keys, values=values, out_grad=out_grad, segments=segments)


def tile_backward(query, key_rows, value_rows, grad_out, allowed):
    row_count = query.shape[0]
    key_count = key_rows.shape[0]
    kv_heads = key_rows.shape[1] // DH
    group_size = query.shape[1] // (kv_heads * DH)
    score_scale = DH ** -0.5
    query_heads = query.reshape(row_count, kv_heads, group_size, DH).astype(jnp.float32)
    grad_heads = grad_out.reshape(row_count, kv_heads, group_size, DH).astype(jnp.float32)
    key_heads = key_rows.reshape(key_count, kv_heads, DH).astype(jnp.float32)
    value_heads = value_rows.reshape(key_count, kv_heads, DH).astype(jnp.float32)
    scores = jnp.einsum("qhgd,khd->hgqk", query_heads, key_heads) * score_scale
    masked = jnp.where(allowed, scores, -jnp.inf)
    row_max = jnp.max(masked, axis=-1, keepdims=True)
    weights = jnp.exp(masked - row_max)
    probability = weights / jnp.sum(weights, axis=-1, keepdims=True)
    prob_low = lax.optimization_barrier(probability.astype(jnp.bfloat16)).astype(jnp.float32)
    output = jnp.einsum("hgqk,khd->qhgd", prob_low, value_heads)
    grad_prob = jnp.einsum("qhgd,khd->hgqk", grad_heads, value_heads)
    grad_dot = jnp.transpose(jnp.sum(grad_heads * output, axis=-1), (1, 2, 0))[..., None]
    grad_score = probability * (grad_prob - grad_dot)
    grad_score = lax.optimization_barrier(grad_score.astype(jnp.bfloat16)).astype(jnp.float32)
    query_grad = jnp.einsum("hgqk,khd->qhgd", grad_score, key_heads) * score_scale
    key_grad = jnp.einsum("hgqk,qhgd->khd", grad_score, query_heads) * score_scale
    value_grad = jnp.einsum("hgqk,qhgd->khd", prob_low, grad_heads)
    return query_grad.reshape(row_count, -1), key_grad.reshape(key_count, -1), value_grad.reshape(key_count, -1)


def make_mask(seg_padded, block_index, row_count):
    query_pos = block_index * row_count + jnp.arange(row_count, dtype=jnp.int32)
    key_pos = block_index * row_count - row_count + jnp.arange(2 * row_count, dtype=jnp.int32)
    seg_query = lax.dynamic_slice_in_dim(seg_padded, block_index * row_count + row_count, row_count)
    seg_key = lax.dynamic_slice_in_dim(seg_padded, block_index * row_count, 2 * row_count)
    near = (key_pos[None, :] <= query_pos[:, None]) & (query_pos[:, None] - key_pos[None, :] < WINDOW)
    return near & (key_pos[None, :] >= 0) & (seg_query[:, None] == seg_key[None, :])


def layer_backward(query_all, key_all, value_all, grad_all, seg_padded):
    row_count = TOK_DEV
    key_padded = jnp.concatenate([jnp.zeros((row_count, key_all.shape[1]), key_all.dtype), key_all], axis=0)
    value_padded = jnp.concatenate([jnp.zeros((row_count, value_all.shape[1]), value_all.dtype), value_all], axis=0)

    def block_grads(block_index):
        query = lax.dynamic_slice_in_dim(query_all, block_index * row_count, row_count)
        grad_out = lax.dynamic_slice_in_dim(grad_all, block_index * row_count, row_count)
        key_rows = lax.dynamic_slice_in_dim(key_padded, block_index * row_count, 2 * row_count)
        value_rows = lax.dynamic_slice_in_dim(value_padded, block_index * row_count, 2 * row_count)
        allowed = make_mask(seg_padded, block_index, row_count)
        return tile_backward(query, key_rows, value_rows, grad_out, allowed)

    query_grad, key_pair, value_pair = lax.map(block_grads, jnp.arange(N_SEQ, dtype=jnp.int32))

    def combine(pair):
        later = jnp.concatenate([pair[1:, :row_count], jnp.zeros_like(pair[:1, :row_count])], axis=0)
        return (pair[:, row_count:] + later).reshape(TOKENS, -1).astype(jnp.bfloat16)

    return query_grad.reshape(TOKENS, -1), combine(key_pair), combine(value_pair)


def reference(queries, keys, values, out_grad, segments):
    query_out = [[None] * MICRO for section_index in range(SECTIONS)]
    key_out = [[None] * MICRO for section_index in range(SECTIONS)]
    value_out = [[None] * MICRO for section_index in range(SECTIONS)]
    for batch_index in range(MICRO):
        seg_padded = jnp.concatenate([jnp.full((TOK_DEV,), -1, jnp.int32), segments[batch_index].astype(jnp.int32)])
        current = out_grad[batch_index]
        for section_index in reversed(range(SECTIONS)):
            query_grad, key_grad, value_grad = layer_backward(queries[section_index, batch_index], keys[section_index, batch_index], values[section_index, batch_index], current, seg_padded)
            current = (current.astype(jnp.float32) + query_grad).astype(jnp.bfloat16)
            query_out[section_index][batch_index] = current
            key_out[section_index][batch_index] = key_grad
            value_out[section_index][batch_index] = value_grad

    def stacked(nested):
        return jnp.stack([jnp.stack(inner) for inner in nested])

    return (stacked(query_out), stacked(key_out), stacked(value_out))
```

```python
import functools

import jax
import jax.numpy as jnp
from jax import lax
from jax.experimental import pallas as pl
from jax.experimental.pallas import tpu as pltpu
from jax.sharding import PartitionSpec as P

DH = 128
LOG2E = 1.4426950408889634
MESH = pl.DeviceIdType.MESH
CHUNK = 2

NT = (((1,), (1,)), ((), ()))
TN = (((0,), (0,)), ((), ()))
NN = (((1,), (0,)), ((), ()))


def dot(left, right, dims):
    return lax.dot_general(left, right, dims, preferred_element_type=jnp.float32)


def stack_heads(rows):
    count = rows.shape[1] // DH
    return jnp.concatenate([rows[:, i * DH : (i + 1) * DH] for i in range(count)], axis=0)


def kernel(
    sections,
    seq_size,
    kv_heads,
    group,
    q_hbm,
    k_hbm,
    v_hbm,
    g_hbm,
    seg_ref,
    qg_hbm,
    kg_hbm,
    vg_hbm,
    x_buf,
    kv_buf,
    prob_buf,
    g_in,
    g_out,
    part_own,
    part_send,
    part_recv,
    kv_out,
    bias_ref,
    pick_ref,
    x_sem,
    own_sem,
    halo_send,
    halo_recv,
    g_send,
    g_recv,
    part_send_sem,
    part_recv_sem,
    qg_sem,
    kvg_sem,
):
    section = lax.axis_index("pipe")
    block = lax.axis_index("seq")
    micro = q_hbm.shape[1]
    items = micro * kv_heads
    per_item = group // CHUNK
    wide = CHUNK * DH
    scale = DH**-0.5
    last = section == sections - 1
    has_next = section > 0
    has_left = block > 0
    has_right = block < seq_size - 1

    def place(item):
        return item // kv_heads, pl.multiple_of(lax.rem(item, kv_heads) * DH, DH)

    def loop(count, body):
        def step(i, carry):
            body(i)
            return carry

        lax.fori_loop(0, count, step, 0)

    def own_copies(item):
        b, col = place(item)
        return (
            pltpu.make_async_copy(
                k_hbm.at[0, b, :, pl.ds(col, DH)], kv_buf.at[item, 0, 1], own_sem.at[item, 0]
            ),
            pltpu.make_async_copy(
                v_hbm.at[0, b, :, pl.ds(col, DH)], kv_buf.at[item, 1, 1], own_sem.at[item, 1]
            ),
            pltpu.make_async_copy(
                q_hbm.at[0, b, :, pl.ds(pl.multiple_of(col * group, DH), group * DH)],
                x_buf.at[item],
                x_sem.at[item],
            ),
        )

    def halo_copies(item):
        b, col = place(item)
        return tuple(
            pltpu.make_async_remote_copy(
                src_ref=ref.at[0, b, :, pl.ds(col, DH)],
                dst_ref=kv_buf.at[item, i, 0],
                send_sem=halo_send.at[item, i],
                recv_sem=halo_recv.at[item, i],
                device_id=(section, block + 1),
                device_id_type=MESH,
            )
            for i, ref in enumerate((k_hbm, v_hbm))
        )

    def grad_copy(chunk):
        return pltpu.make_async_remote_copy(
            src_ref=g_out.at[chunk],
            dst_ref=g_in.at[chunk],
            send_sem=g_send.at[chunk],
            recv_sem=g_recv.at[chunk],
            device_id=(section - 1, block),
            device_id_type=MESH,
        )

    def top_copy(chunk):
        per_micro = kv_heads * per_item
        col = pl.multiple_of(lax.rem(chunk, per_micro) * wide, DH)
        return pltpu.make_async_copy(
            g_hbm.at[chunk // per_micro, :, pl.ds(col, wide)], g_in.at[chunk], g_recv.at[chunk]
        )

    def out_copy(chunk):
        per_micro = kv_heads * per_item
        col = pl.multiple_of(lax.rem(chunk, per_micro) * wide, DH)
        return pltpu.make_async_copy(
            g_out.at[chunk],
            qg_hbm.at[0, chunk // per_micro, :, pl.ds(col, wide)],
            qg_sem.at[chunk],
        )

    def part_copy(item):
        return pltpu.make_async_remote_copy(
            src_ref=part_send.at[item],
            dst_ref=part_recv.at[item],
            send_sem=part_send_sem.at[item],
            recv_sem=part_recv_sem.at[item],
            device_id=(section, block - 1),
            device_id_type=MESH,
        )

    def kv_out_copies(item):
        b, col = place(item)
        return tuple(
            pltpu.make_async_copy(
                kv_out.at[item, i], ref.at[0, b, :, pl.ds(col, DH)], kvg_sem.at[item, i]
            )
            for i, ref in enumerate((kg_hbm, vg_hbm))
        )

    barrier = pltpu.get_barrier_semaphore()
    neighbours = (
        (has_next, (section - 1, block)),
        (section < sections - 1, (section + 1, block)),
        (has_left, (section, block - 1)),
        (has_right, (section, block + 1)),
    )
    for exists, device in neighbours:

        @pl.when(exists)
        def _(device=device):
            pl.semaphore_signal(barrier, inc=1, device_id=device, device_id_type=MESH)

    def start_own(item):
        for copy in own_copies(item):
            copy.start()

    loop(items, start_own)

    @pl.when(last)
    def _():
        loop(items * per_item, lambda chunk: top_copy(chunk).start())

    @pl.when(jnp.logical_not(has_left))
    def _():
        def clear(item):
            for i in range(2):
                kv_buf[item, i, 0] = jnp.zeros((DH, DH), jnp.bfloat16)

        loop(items, clear)

    @pl.when(jnp.logical_not(has_right))
    def _():
        def clear(item):
            part_recv[item] = jnp.zeros(part_recv.shape[1:], jnp.bfloat16)

        loop(items, clear)

    key_at = lax.broadcasted_iota(jnp.int32, (DH, DH), 0)
    query_at = lax.broadcasted_iota(jnp.int32, (DH, DH), 1)
    in_own = key_at <= query_at
    before = jnp.maximum(block - 1, 0)
    for b in range(micro):
        seg_query = seg_ref[b : b + 1, pl.ds(pl.multiple_of(block * DH, DH), DH)]
        seg_halo = seg_ref[b : b + 1, pl.ds(pl.multiple_of(before * DH, DH), DH)]
        seg_query = jnp.broadcast_to(seg_query.astype(jnp.float32), (DH, DH))
        seg_halo = jnp.broadcast_to(seg_halo.astype(jnp.float32), (DH, DH))
        seg_halo = jnp.where(has_left, seg_halo, -1.0)
        seg_key = jnp.where(in_own, seg_query.T, seg_halo.T)
        bias_ref[b] = jnp.where(seg_key == seg_query, 0.0, -1e30)
    pick_ref[0] = jnp.where(in_own, 0.0, 1.0).astype(jnp.bfloat16)
    pick_ref[1] = jnp.where(in_own, 1.0, 0.0).astype(jnp.bfloat16)

    pl.semaphore_wait(barrier, sum(exists.astype(jnp.int32) for exists, _ in neighbours))

    @pl.when(has_right)
    def _():
        def send_halo(item):
            for copy in halo_copies(item):
                copy.start()

        loop(items, send_halo)

    def merge(both):
        count = both.shape[1] // DH
        keep = jnp.concatenate([in_own] * count, axis=1)
        return jnp.where(keep, both[DH:], both[:DH])

    def spread(packed):
        count = packed.shape[1] // DH
        return jnp.concatenate(
            [jnp.concatenate([pick_ref[i]] * count, axis=1) * packed for i in range(2)], axis=0
        )

    def probabilities(item):
        for copy in own_copies(item):
            copy.wait()

        @pl.when(has_left)
        def _():
            for copy in halo_copies(item):
                copy.wait_recv()

        key = kv_buf[item, 0].reshape(2 * DH, DH)
        bias = bias_ref[item // kv_heads]
        for part in range(per_item):
            cols = slice(part * wide, (part + 1) * wide)
            query = stack_heads(x_buf[item, :, cols])
            score = merge(dot(key, query, NT)) + jnp.concatenate([bias] * CHUNK, axis=1)
            top = jnp.max(score, axis=0, keepdims=True)
            weight = jnp.exp2((score - top) * (scale * LOG2E))
            total = jnp.sum(weight, axis=0, keepdims=True)
            prob_buf[item, :, cols] = weight * (1.0 / total)

    @pl.when(jnp.logical_not(last))
    def _():
        loop(items, probabilities)

    def backward(item):
        @pl.when(last)
        def _():
            probabilities(item)

        key = kv_buf[item, 0].reshape(2 * DH, DH)
        value = kv_buf[item, 1].reshape(2 * DH, DH)
        key_grad = value_grad = None
        for part in range(per_item):
            chunk = item * per_item + part
            pltpu.make_async_copy(g_in.at[chunk], g_in.at[chunk], g_recv.at[chunk]).wait()
            cols = slice(part * wide, (part + 1) * wide)
            query = stack_heads(x_buf[item, :, cols])
            grad = stack_heads(g_in[chunk])
            prob = prob_buf[item, :, cols]
            prob_low = prob.astype(jnp.bfloat16)
            grad_prob = merge(dot(value, grad, NT))
            delta = jnp.sum(prob_low.astype(jnp.float32) * grad_prob, axis=0, keepdims=True)
            grad_score = spread((prob * (grad_prob - delta)).astype(jnp.bfloat16))
            query_grad = dot(grad_score, key, TN) * scale
            grad_next = (grad.astype(jnp.float32) + query_grad).astype(jnp.bfloat16)
            for i in range(CHUNK):
                g_out[chunk, :, i * DH : (i + 1) * DH] = grad_next[i * DH : (i + 1) * DH]

            @pl.when(has_next)
            def _():
                grad_copy(chunk).start()

            out_copy(chunk).start()
            key_part = dot(grad_score, query, NN)
            value_part = dot(spread(prob_low), grad, NN)
            key_grad = key_part if part == 0 else key_grad + key_part
            value_grad = value_part if part == 0 else value_grad + value_part
        for i, total in enumerate((key_grad * scale, value_grad)):
            part_send[item, i] = total[:DH].astype(jnp.bfloat16)
            part_own[item, i] = total[DH:]

        @pl.when(has_left)
        def _():
            part_copy(item).start()

    loop(items, backward)

    def finish(item):
        @pl.when(has_right)
        def _():
            part_copy(item).wait_recv()

        total = part_own[item] + part_recv[item].astype(jnp.float32)
        kv_out[item] = total.astype(jnp.bfloat16)
        for copy in kv_out_copies(item):
            copy.start()

    loop(items, finish)

    def drain(item):
        for copy in kv_out_copies(item):
            copy.wait()
        for part in range(per_item):
            chunk = item * per_item + part
            out_copy(chunk).wait()

            @pl.when(has_next)
            def _():
                grad_copy(chunk).wait_send()

        @pl.when(has_right)
        def _():
            for copy in halo_copies(item):
                copy.wait_send()

        @pl.when(has_left)
        def _():
            part_copy(item).wait_send()

    loop(items, drain)


def per_device(sections, seq_size, queries, keys, values, out_grad, segments):
    micro, rows, query_width = queries.shape[1:]
    key_width = keys.shape[3]
    kv_heads = key_width // DH
    group = query_width // key_width
    items = micro * kv_heads
    chunks = items * group // CHUNK
    anywhere = pl.BlockSpec(memory_space=pl.ANY)
    low, full = jnp.bfloat16, jnp.float32
    dma = pltpu.SemaphoreType.DMA
    return pl.pallas_call(
        functools.partial(kernel, sections, seq_size, kv_heads, group),
        out_shape=(
            jax.ShapeDtypeStruct(queries.shape, low),
            jax.ShapeDtypeStruct(keys.shape, low),
            jax.ShapeDtypeStruct(values.shape, low),
        ),
        in_specs=[anywhere] * 4 + [pl.BlockSpec(memory_space=pltpu.VMEM)],
        out_specs=(anywhere,) * 3,
        scratch_shapes=[
            pltpu.VMEM((items, rows, group * DH), low),
            pltpu.VMEM((items, 2, 2, rows, DH), low),
            pltpu.VMEM((items, rows, group * DH), full),
            pltpu.VMEM((chunks, rows, CHUNK * DH), low),
            pltpu.VMEM((chunks, rows, CHUNK * DH), low),
            pltpu.VMEM((items, 2, rows, DH), full),
            pltpu.VMEM((items, 2, rows, DH), low),
            pltpu.VMEM((items, 2, rows, DH), low),
            pltpu.VMEM((items, 2, rows, DH), low),
            pltpu.VMEM((micro, DH, DH), full),
            pltpu.VMEM((2, DH, DH), low),
            dma((items,)),
            dma((items, 2)),
            dma((items, 2)),
            dma((items, 2)),
            dma((chunks,)),
            dma((chunks,)),
            dma((items,)),
            dma((items,)),
            dma((chunks,)),
            dma((items, 2)),
        ],
        compiler_params=pltpu.CompilerParams(
            collective_id=0, has_side_effects=True, vmem_limit_bytes=40 * 1024 * 1024
        ),
        cost_estimate=pl.CostEstimate(
            flops=10 * items * group * rows * 2 * rows * DH,
            bytes_accessed=6 * 1024 * 1024,
            transcendentals=items * group * rows * rows,
        ),
    )(queries, keys, values, out_grad, segments)


def solution(mesh):
    sizes = dict(mesh.shape)
    split = P("pipe", None, "seq", None)
    return jax.shard_map(
        functools.partial(per_device, sizes["pipe"], sizes["seq"]),
        mesh=mesh,
        in_specs=(split, split, split, P(None, "seq", None), P()),
        out_specs=(split, split, split),
        check_vma=False,
    )
```

```python
import functools

import jax
import jax.numpy as jnp
from jax import lax
from jax.experimental import pallas as pl
from jax.experimental.pallas import tpu as pltpu
from jax.sharding import PartitionSpec as P

DH = 128
LOG2E = 1.4426950408889634
MESH = pl.DeviceIdType.MESH
CHUNK = 1

NT = (((1,), (1,)), ((), ()))
TN = (((0,), (0,)), ((), ()))
NN = (((1,), (0,)), ((), ()))


def dot(left, right, dims):
    return lax.dot_general(left, right, dims, preferred_element_type=jnp.float32)


def stack_heads(rows):
    count = rows.shape[1] // DH
    return jnp.concatenate([rows[:, i * DH : (i + 1) * DH] for i in range(count)], axis=0)


def kernel(
    sections,
    seq_size,
    kv_heads,
    group,
    q_hbm,
    k_hbm,
    v_hbm,
    g_hbm,
    seg_hbm,
    qg_hbm,
    kg_hbm,
    vg_hbm,
    x_buf,
    kv_buf,
    prob_buf,
    ds_buf,
    g_in,
    g_out,
    part_own,
    part_send,
    part_recv,
    kv_out,
    bias_ref,
    pick_ref,
    seg_ref,
    seg_sem,
    x_sem,
    own_sem,
    halo_send,
    halo_recv,
    g_send,
    g_recv,
    part_send_sem,
    part_recv_sem,
    qg_sem,
    kvg_sem,
):
    section = lax.axis_index("pipe")
    block = lax.axis_index("seq")
    micro = q_hbm.shape[1]
    items = micro * kv_heads
    per_item = group // CHUNK
    wide = CHUNK * DH
    scale = DH**-0.5
    last = section == sections - 1
    has_next = section > 0
    has_left = block > 0
    has_right = block < seq_size - 1

    def place(item):
        return item // kv_heads, pl.multiple_of(lax.rem(item, kv_heads) * DH, DH)

    def loop(count, body):
        def step(i, carry):
            body(i)
            return carry

        lax.fori_loop(0, count, step, 0)

    def own_copies(item):
        b, col = place(item)
        return (
            pltpu.make_async_copy(
                k_hbm.at[0, b, :, pl.ds(col, DH)], kv_buf.at[item, 0, 1], own_sem.at[item, 0]
            ),
            pltpu.make_async_copy(
                v_hbm.at[0, b, :, pl.ds(col, DH)], kv_buf.at[item, 1, 1], own_sem.at[item, 1]
            ),
            pltpu.make_async_copy(
                q_hbm.at[0, b, :, pl.ds(pl.multiple_of(col * group, DH), group * DH)],
                x_buf.at[item],
                x_sem.at[item],
            ),
        )

    def halo_copies(item):
        b, col = place(item)
        return tuple(
            pltpu.make_async_remote_copy(
                src_ref=ref.at[0, b, :, pl.ds(col, DH)],
                dst_ref=kv_buf.at[item, i, 0],
                send_sem=halo_send.at[item, i],
                recv_sem=halo_recv.at[item, i],
                device_id=(section, block + 1),
                device_id_type=MESH,
            )
            for i, ref in enumerate((k_hbm, v_hbm))
        )

    def grad_copy(chunk):
        return pltpu.make_async_remote_copy(
            src_ref=g_out.at[chunk],
            dst_ref=g_in.at[chunk],
            send_sem=g_send.at[chunk],
            recv_sem=g_recv.at[chunk],
            device_id=(section - 1, block),
            device_id_type=MESH,
        )

    def top_copy(chunk):
        per_micro = kv_heads * per_item
        col = pl.multiple_of(lax.rem(chunk, per_micro) * wide, DH)
        return pltpu.make_async_copy(
            g_hbm.at[chunk // per_micro, :, pl.ds(col, wide)], g_in.at[chunk], g_recv.at[chunk]
        )

    def out_copy(chunk):
        per_micro = kv_heads * per_item
        col = pl.multiple_of(lax.rem(chunk, per_micro) * wide, DH)
        return pltpu.make_async_copy(
            g_out.at[chunk],
            qg_hbm.at[0, chunk // per_micro, :, pl.ds(col, wide)],
            qg_sem.at[chunk],
        )

    def part_copy(item):
        return pltpu.make_async_remote_copy(
            src_ref=part_send.at[item],
            dst_ref=part_recv.at[item],
            send_sem=part_send_sem.at[item],
            recv_sem=part_recv_sem.at[item],
            device_id=(section, block - 1),
            device_id_type=MESH,
        )

    def kv_out_copies(item):
        b, col = place(item)
        return tuple(
            pltpu.make_async_copy(
                kv_out.at[item, i], ref.at[0, b, :, pl.ds(col, DH)], kvg_sem.at[item, i]
            )
            for i, ref in enumerate((kg_hbm, vg_hbm))
        )

    barrier = pltpu.get_barrier_semaphore()
    neighbours = (
        (has_next, (section - 1, block)),
        (section < sections - 1, (section + 1, block)),
        (has_left, (section, block - 1)),
        (has_right, (section, block + 1)),
    )
    for exists, device in neighbours:

        @pl.when(exists)
        def _(device=device):
            pl.semaphore_signal(barrier, inc=1, device_id=device, device_id_type=MESH)

    seg_copy = pltpu.make_async_copy(seg_hbm, seg_ref, seg_sem)
    seg_copy.start()

    def start_own(item):
        for copy in own_copies(item):
            copy.start()

    loop(items, start_own)

    pl.semaphore_wait(barrier, sum(exists.astype(jnp.int32) for exists, _ in neighbours))

    @pl.when(has_right)
    def _():
        def send_halo(item):
            for copy in halo_copies(item):
                copy.start()

        loop(items, send_halo)

    @pl.when(last)
    def _():
        loop(items * per_item, lambda chunk: top_copy(chunk).start())

    @pl.when(jnp.logical_not(has_left))
    def _():
        def clear(item):
            for i in range(2):
                kv_buf[item, i, 0] = jnp.zeros((DH, DH), jnp.bfloat16)

        loop(items, clear)

    @pl.when(jnp.logical_not(has_right))
    def _():
        def clear(item):
            part_recv[item] = jnp.zeros(part_recv.shape[1:], jnp.bfloat16)

        loop(items, clear)

    key_at = lax.broadcasted_iota(jnp.int32, (DH, DH), 0)
    query_at = lax.broadcasted_iota(jnp.int32, (DH, DH), 1)
    in_own = key_at <= query_at
    before = jnp.maximum(block - 1, 0)
    seg_copy.wait()
    for b in range(micro):
        seg_query = seg_ref[b : b + 1, pl.ds(pl.multiple_of(block * DH, DH), DH)]
        seg_halo = seg_ref[b : b + 1, pl.ds(pl.multiple_of(before * DH, DH), DH)]
        seg_query = jnp.broadcast_to(seg_query.astype(jnp.float32), (DH, DH))
        seg_halo = jnp.broadcast_to(seg_halo.astype(jnp.float32), (DH, DH))
        seg_halo = jnp.where(has_left, seg_halo, -1.0)
        seg_key = jnp.where(in_own, seg_query.T, seg_halo.T)
        bias_ref[b] = jnp.where(seg_key == seg_query, 0.0, -1e30)
    pick_ref[0] = jnp.where(in_own, 0.0, 1.0).astype(jnp.bfloat16)
    pick_ref[1] = jnp.where(in_own, 1.0, 0.0).astype(jnp.bfloat16)

    def merge(both):
        count = both.shape[1] // DH
        keep = jnp.concatenate([in_own] * count, axis=1)
        return jnp.where(keep, both[DH:], both[:DH])

    def spread(packed):
        count = packed.shape[1] // DH
        return jnp.concatenate(
            [jnp.concatenate([pick_ref[i]] * count, axis=1) * packed for i in range(2)], axis=0
        )

    def probabilities(item):
        for copy in own_copies(item):
            copy.wait()

        @pl.when(has_left)
        def _():
            for copy in halo_copies(item):
                copy.wait_recv()

        key = kv_buf[item, 0].reshape(2 * DH, DH)
        bias = bias_ref[item // kv_heads]
        query = stack_heads(x_buf[item])
        score = merge(dot(key, query, NT)) + jnp.concatenate([bias] * group, axis=1)
        top = jnp.max(score, axis=0, keepdims=True)
        weight = jnp.exp2((score - top) * (scale * LOG2E))
        total = jnp.sum(weight, axis=0, keepdims=True)
        prob_buf[item] = weight * (1.0 / total)

    @pl.when(jnp.logical_not(last))
    def _():
        loop(items, probabilities)

    def key_value_grads(item):
        query = stack_heads(x_buf[item])
        grad = jnp.concatenate(
            [stack_heads(g_in[item * per_item + part]) for part in range(per_item)], axis=0
        )
        key_grad = dot(ds_buf[item], query, NN) * scale
        value_grad = dot(spread(prob_buf[item].astype(jnp.bfloat16)), grad, NN)
        for i, total in enumerate((key_grad, value_grad)):
            part_send[item, i] = total[:DH].astype(jnp.bfloat16)
            part_own[item, i] = total[DH:]

        @pl.when(has_left)
        def _():
            part_copy(item).start()

    def backward(item):
        @pl.when(last)
        def _():
            probabilities(item)

        key = kv_buf[item, 0].reshape(2 * DH, DH)
        value = kv_buf[item, 1].reshape(2 * DH, DH)
        for part in range(per_item):
            chunk = item * per_item + part
            pltpu.make_async_copy(g_in.at[chunk], g_in.at[chunk], g_recv.at[chunk]).wait()
            cols = slice(part * wide, (part + 1) * wide)
            grad = stack_heads(g_in[chunk])
            prob = prob_buf[item, :, cols]
            prob_low = prob.astype(jnp.bfloat16)
            grad_prob = merge(dot(value, grad, NT))
            delta = jnp.sum(prob_low.astype(jnp.float32) * grad_prob, axis=0, keepdims=True)
            grad_score = spread((prob * (grad_prob - delta)).astype(jnp.bfloat16))
            ds_buf[item, :, cols] = grad_score
            query_grad = dot(grad_score, key, TN) * scale
            grad_next = (grad.astype(jnp.float32) + query_grad).astype(jnp.bfloat16)
            for i in range(CHUNK):
                g_out[chunk, :, i * DH : (i + 1) * DH] = grad_next[i * DH : (i + 1) * DH]

            @pl.when(has_next)
            def _():
                grad_copy(chunk).start()

            out_copy(chunk).start()

        @pl.when(jnp.logical_not(has_next))
        def _():
            key_value_grads(item)

    loop(items, backward)

    @pl.when(has_next)
    def _():
        loop(items, key_value_grads)

    def finish(item):
        @pl.when(has_right)
        def _():
            part_copy(item).wait_recv()

        total = part_own[item] + part_recv[item].astype(jnp.float32)
        kv_out[item] = total.astype(jnp.bfloat16)
        for copy in kv_out_copies(item):
            copy.start()

    loop(items, finish)

    def drain(item):
        for copy in kv_out_copies(item):
            copy.wait()
        for part in range(per_item):
            chunk = item * per_item + part
            out_copy(chunk).wait()

            @pl.when(has_next)
            def _():
                grad_copy(chunk).wait_send()

        @pl.when(has_right)
        def _():
            for copy in halo_copies(item):
                copy.wait_send()

        @pl.when(has_left)
        def _():
            part_copy(item).wait_send()

    loop(items, drain)


def per_device(sections, seq_size, queries, keys, values, out_grad, segments):
    micro, rows, query_width = queries.shape[1:]
    key_width = keys.shape[3]
    kv_heads = key_width // DH
    group = query_width // key_width
    items = micro * kv_heads
    chunks = items * group // CHUNK
    anywhere = pl.BlockSpec(memory_space=pl.ANY)
    low, full = jnp.bfloat16, jnp.float32
    dma = pltpu.SemaphoreType.DMA
    return pl.pallas_call(
        functools.partial(kernel, sections, seq_size, kv_heads, group),
        out_shape=(
            jax.ShapeDtypeStruct(queries.shape, low),
            jax.ShapeDtypeStruct(keys.shape, low),
            jax.ShapeDtypeStruct(values.shape, low),
        ),
        in_specs=[anywhere] * 5,
        out_specs=(anywhere,) * 3,
        scratch_shapes=[
            pltpu.VMEM((items, rows, group * DH), low),
            pltpu.VMEM((items, 2, 2, rows, DH), low),
            pltpu.VMEM((items, rows, group * DH), full),
            pltpu.VMEM((items, 2 * rows, group * DH), low),
            pltpu.VMEM((chunks, rows, CHUNK * DH), low),
            pltpu.VMEM((chunks, rows, CHUNK * DH), low),
            pltpu.VMEM((items, 2, rows, DH), full),
            pltpu.VMEM((items, 2, rows, DH), low),
            pltpu.VMEM((items, 2, rows, DH), low),
            pltpu.VMEM((items, 2, rows, DH), low),
            pltpu.VMEM((micro, DH, DH), full),
            pltpu.VMEM((2, DH, DH), low),
            pltpu.VMEM(segments.shape, jnp.int32),
            dma(()),
            dma((items,)),
            dma((items, 2)),
            dma((items, 2)),
            dma((items, 2)),
            dma((chunks,)),
            dma((chunks,)),
            dma((items,)),
            dma((items,)),
            dma((chunks,)),
            dma((items, 2)),
        ],
        compiler_params=pltpu.CompilerParams(
            collective_id=0, has_side_effects=True, vmem_limit_bytes=60 * 1024 * 1024
        ),
        cost_estimate=pl.CostEstimate(
            flops=10 * items * group * rows * 2 * rows * DH,
            bytes_accessed=6 * 1024 * 1024,
            transcendentals=items * group * rows * rows,
        ),
    )(queries, keys, values, out_grad, segments)


def solution(mesh):
    sizes = dict(mesh.shape)
    split = P("pipe", None, "seq", None)
    return jax.shard_map(
        functools.partial(per_device, sizes["pipe"], sizes["seq"]),
        mesh=mesh,
        in_specs=(split, split, split, P(None, "seq", None), P()),
        out_specs=(split, split, split),
        check_vma=False,
    )
```

```python
import functools

import jax
import jax.numpy as jnp
from jax import lax
from jax.experimental import pallas as pl
from jax.experimental.pallas import tpu as pltpu
from jax.sharding import PartitionSpec as P

DH = 128
LOG2E = 1.4426950408889634
MESH = pl.DeviceIdType.MESH
CHUNK = 2

NT = (((1,), (1,)), ((), ()))
TN = (((0,), (0,)), ((), ()))
NN = (((1,), (0,)), ((), ()))


def dot(left, right, dims):
    return lax.dot_general(left, right, dims, preferred_element_type=jnp.float32)


def stack_heads(rows):
    count = rows.shape[1] // DH
    return jnp.concatenate([rows[:, i * DH : (i + 1) * DH] for i in range(count)], axis=0)


def kernel(
    sections,
    seq_size,
    kv_heads,
    group,
    q_hbm,
    k_hbm,
    v_hbm,
    g_hbm,
    seg_hbm,
    qg_hbm,
    kg_hbm,
    vg_hbm,
    x_buf,
    kv_buf,
    prob_buf,
    ds_buf,
    g_in,
    g_out,
    part_own,
    part_send,
    part_recv,
    kv_out,
    bias_ref,
    pick_ref,
    seg_ref,
    seg_sem,
    x_sem,
    own_sem,
    halo_send,
    halo_recv,
    g_send,
    g_recv,
    part_send_sem,
    part_recv_sem,
    qg_sem,
    kvg_sem,
):
    section = lax.axis_index("pipe")
    block = lax.axis_index("seq")
    micro = q_hbm.shape[1]
    items = micro * kv_heads
    per_item = group // CHUNK
    wide = CHUNK * DH
    scale = DH**-0.5
    last = section == sections - 1
    has_next = section > 0
    has_left = block > 0
    has_right = block < seq_size - 1

    def place(item):
        return item // kv_heads, pl.multiple_of(lax.rem(item, kv_heads) * DH, DH)

    def loop(count, body):
        def step(i, carry):
            body(i)
            return carry

        lax.fori_loop(0, count, step, 0)

    def own_copies(item):
        b, col = place(item)
        return (
            pltpu.make_async_copy(
                k_hbm.at[0, b, :, pl.ds(col, DH)], kv_buf.at[item, 0, 1], own_sem.at[item, 0]
            ),
            pltpu.make_async_copy(
                v_hbm.at[0, b, :, pl.ds(col, DH)], kv_buf.at[item, 1, 1], own_sem.at[item, 1]
            ),
            pltpu.make_async_copy(
                q_hbm.at[0, b, :, pl.ds(pl.multiple_of(col * group, DH), group * DH)],
                x_buf.at[item],
                x_sem.at[item],
            ),
        )

    def halo_copies(item):
        b, col = place(item)
        return tuple(
            pltpu.make_async_remote_copy(
                src_ref=ref.at[0, b, :, pl.ds(col, DH)],
                dst_ref=kv_buf.at[item, i, 0],
                send_sem=halo_send.at[item, i],
                recv_sem=halo_recv.at[item, i],
                device_id=(section, block + 1),
                device_id_type=MESH,
            )
            for i, ref in enumerate((k_hbm, v_hbm))
        )

    def grad_copy(chunk):
        return pltpu.make_async_remote_copy(
            src_ref=g_out.at[chunk],
            dst_ref=g_in.at[chunk],
            send_sem=g_send.at[chunk],
            recv_sem=g_recv.at[chunk],
            device_id=(section - 1, block),
            device_id_type=MESH,
        )

    def top_copy(chunk):
        per_micro = kv_heads * per_item
        col = pl.multiple_of(lax.rem(chunk, per_micro) * wide, DH)
        return pltpu.make_async_copy(
            g_hbm.at[chunk // per_micro, :, pl.ds(col, wide)], g_in.at[chunk], g_recv.at[chunk]
        )

    def out_copy(chunk):
        per_micro = kv_heads * per_item
        col = pl.multiple_of(lax.rem(chunk, per_micro) * wide, DH)
        return pltpu.make_async_copy(
            g_out.at[chunk],
            qg_hbm.at[0, chunk // per_micro, :, pl.ds(col, wide)],
            qg_sem.at[chunk],
        )

    def part_copy(item):
        return pltpu.make_async_remote_copy(
            src_ref=part_send.at[item],
            dst_ref=part_recv.at[item],
            send_sem=part_send_sem.at[item],
            recv_sem=part_recv_sem.at[item],
            device_id=(section, block - 1),
            device_id_type=MESH,
        )

    def kv_out_copies(item):
        b, col = place(item)
        return tuple(
            pltpu.make_async_copy(
                kv_out.at[item, i], ref.at[0, b, :, pl.ds(col, DH)], kvg_sem.at[item, i]
            )
            for i, ref in enumerate((kg_hbm, vg_hbm))
        )

    barrier = pltpu.get_barrier_semaphore()
    neighbours = (
        (has_next, (section - 1, block)),
        (section < sections - 1, (section + 1, block)),
        (has_left, (section, block - 1)),
        (has_right, (section, block + 1)),
    )
    for exists, device in neighbours:

        @pl.when(exists)
        def _(device=device):
            pl.semaphore_signal(barrier, inc=1, device_id=device, device_id_type=MESH)

    seg_copy = pltpu.make_async_copy(seg_hbm, seg_ref, seg_sem)
    seg_copy.start()

    def start_own(item):
        for copy in own_copies(item):
            copy.start()

    loop(items, start_own)

    pl.semaphore_wait(barrier, sum(exists.astype(jnp.int32) for exists, _ in neighbours))

    @pl.when(has_right)
    def _():
        def send_halo(item):
            for copy in halo_copies(item):
                copy.start()

        loop(items, send_halo)

    @pl.when(last)
    def _():
        loop(items * per_item, lambda chunk: top_copy(chunk).start())

    @pl.when(jnp.logical_not(has_left))
    def _():
        def clear(item):
            for i in range(2):
                kv_buf[item, i, 0] = jnp.zeros((DH, DH), jnp.bfloat16)

        loop(items, clear)

    @pl.when(jnp.logical_not(has_right))
    def _():
        def clear(item):
            part_recv[item] = jnp.zeros(part_recv.shape[1:], jnp.bfloat16)

        loop(items, clear)

    key_at = lax.broadcasted_iota(jnp.int32, (DH, DH), 0)
    query_at = lax.broadcasted_iota(jnp.int32, (DH, DH), 1)
    in_own = key_at <= query_at
    before = jnp.maximum(block - 1, 0)
    seg_copy.wait()
    for b in range(micro):
        seg_query = seg_ref[b : b + 1, pl.ds(pl.multiple_of(block * DH, DH), DH)]
        seg_halo = seg_ref[b : b + 1, pl.ds(pl.multiple_of(before * DH, DH), DH)]
        seg_query = jnp.broadcast_to(seg_query.astype(jnp.float32), (DH, DH))
        seg_halo = jnp.broadcast_to(seg_halo.astype(jnp.float32), (DH, DH))
        seg_halo = jnp.where(has_left, seg_halo, -1.0)
        seg_key = jnp.where(in_own, seg_query.T, seg_halo.T)
        bias_ref[b] = jnp.where(seg_key == seg_query, 0.0, -1e30)
    pick_ref[0] = jnp.where(in_own, 0.0, 1.0).astype(jnp.bfloat16)
    pick_ref[1] = jnp.where(in_own, 1.0, 0.0).astype(jnp.bfloat16)

    def merge(both):
        count = both.shape[1] // DH
        keep = jnp.concatenate([in_own] * count, axis=1)
        return jnp.where(keep, both[DH:], both[:DH])

    def spread(packed):
        count = packed.shape[1] // DH
        return jnp.concatenate(
            [jnp.concatenate([pick_ref[i]] * count, axis=1) * packed for i in range(2)], axis=0
        )

    def arrive(item):
        for copy in own_copies(item):
            copy.wait()

        @pl.when(has_left)
        def _():
            for copy in halo_copies(item):
                copy.wait_recv()

    def probabilities(item, cols):
        key = kv_buf[item, 0].reshape(2 * DH, DH)
        query = stack_heads(x_buf[item, :, cols])
        bias = jnp.concatenate([bias_ref[item // kv_heads]] * (query.shape[0] // DH), axis=1)
        score = merge(dot(key, query, NT)) + bias
        top = jnp.max(score, axis=0, keepdims=True)
        weight = jnp.exp2((score - top) * (scale * LOG2E))
        total = jnp.sum(weight, axis=0, keepdims=True)
        prob_buf[item, :, cols] = weight * (1.0 / total)

    whole = slice(0, group * DH)

    def store_part(item, i, total):
        part_send[item, i] = total[:DH].astype(jnp.bfloat16)
        part_own[item, i] = total[DH:]

    def key_grad(item):
        query = stack_heads(x_buf[item])
        store_part(item, 0, dot(ds_buf[item], query, NN) * scale)

    def value_grad(item):
        grad = jnp.concatenate(
            [stack_heads(g_in[item * per_item + part]) for part in range(per_item)], axis=0
        )
        store_part(item, 1, dot(spread(prob_buf[item].astype(jnp.bfloat16)), grad, NN))

    def send_part(item):
        @pl.when(has_left)
        def _():
            part_copy(item).start()

    def both_grads(item):
        key_grad(item)
        value_grad(item)
        send_part(item)

    def backward(item, beside):
        key = kv_buf[item, 0].reshape(2 * DH, DH)
        value = kv_buf[item, 1].reshape(2 * DH, DH)
        for part in range(per_item):
            chunk = item * per_item + part
            pltpu.make_async_copy(g_in.at[chunk], g_in.at[chunk], g_recv.at[chunk]).wait()
            cols = slice(part * wide, (part + 1) * wide)
            grad = stack_heads(g_in[chunk])
            prob = prob_buf[item, :, cols]
            prob_low = prob.astype(jnp.bfloat16)
            grad_prob = merge(dot(value, grad, NT))
            delta = jnp.sum(prob_low.astype(jnp.float32) * grad_prob, axis=0, keepdims=True)
            grad_score = spread((prob * (grad_prob - delta)).astype(jnp.bfloat16))
            query_grad = dot(grad_score, key, TN) * scale
            grad_next = (grad.astype(jnp.float32) + query_grad).astype(jnp.bfloat16)
            for i in range(CHUNK):
                g_out[chunk, :, i * DH : (i + 1) * DH] = grad_next[i * DH : (i + 1) * DH]
            beside(part)
            ds_buf[item, :, cols] = grad_score

            @pl.when(has_next)
            def _():
                grad_copy(chunk).start()

            out_copy(chunk).start()

    def nothing(part):
        pass

    @pl.when(last)
    def _():
        arrive(0)
        probabilities(0, whole)

        def one(item):
            arrive(item + 1)

            def ahead(part):
                probabilities(item + 1, slice(part * wide, (part + 1) * wide))

            backward(item, ahead)

        loop(items - 1, one)
        backward(items - 1, nothing)
        loop(items, both_grads)

    @pl.when(jnp.logical_not(last))
    def _():
        def prepare(item):
            arrive(item)
            probabilities(item, whole)

        loop(items, prepare)
        backward(0, nothing)

        def one(i):
            def behind(part):
                if part == 0:
                    key_grad(i)
                if part == per_item - 1:
                    value_grad(i)

            backward(i + 1, behind)
            send_part(i)

        loop(items - 1, one)
        both_grads(items - 1)

    def finish(item):
        @pl.when(has_right)
        def _():
            part_copy(item).wait_recv()

        total = part_own[item] + part_recv[item].astype(jnp.float32)
        kv_out[item] = total.astype(jnp.bfloat16)
        for copy in kv_out_copies(item):
            copy.start()

    loop(items, finish)

    def drain(item):
        for copy in kv_out_copies(item):
            copy.wait()
        for part in range(per_item):
            chunk = item * per_item + part
            out_copy(chunk).wait()

            @pl.when(has_next)
            def _():
                grad_copy(chunk).wait_send()

        @pl.when(has_right)
        def _():
            for copy in halo_copies(item):
                copy.wait_send()

        @pl.when(has_left)
        def _():
            part_copy(item).wait_send()

    loop(items, drain)


def hand_over(pieces, *refs):
    sources, results, sem = refs[:3], refs[3:6], refs[6]
    copies = []
    for i, (source, result) in enumerate(zip(sources, results)):
        rows = source.shape[2] // pieces
        for j in range(pieces):
            at = (0, slice(None), pl.ds(j * rows, rows))
            copies.append(pltpu.make_async_copy(source.at[at], result.at[at], sem.at[i, j]))
    for copy in copies:
        copy.start()
    for copy in copies:
        copy.wait()


def per_device(sections, seq_size, queries, keys, values, out_grad, segments):
    micro, rows, query_width = queries.shape[1:]
    key_width = keys.shape[3]
    kv_heads = key_width // DH
    group = query_width // key_width
    items = micro * kv_heads
    chunks = items * group // CHUNK
    anywhere = pl.BlockSpec(memory_space=pl.ANY)
    low, full = jnp.bfloat16, jnp.float32
    dma = pltpu.SemaphoreType.DMA
    shapes = tuple(jax.ShapeDtypeStruct(x.shape, low) for x in (queries, keys, values))
    grads = pl.pallas_call(
        functools.partial(kernel, sections, seq_size, kv_heads, group),
        out_shape=shapes,
        in_specs=[anywhere] * 5,
        out_specs=(anywhere,) * 3,
        scratch_shapes=[
            pltpu.VMEM((items, rows, group * DH), low),
            pltpu.VMEM((items, 2, 2, rows, DH), low),
            pltpu.VMEM((items, rows, group * DH), full),
            pltpu.VMEM((items, 2 * rows, group * DH), low),
            pltpu.VMEM((chunks, rows, CHUNK * DH), low),
            pltpu.VMEM((chunks, rows, CHUNK * DH), low),
            pltpu.VMEM((items, 2, rows, DH), full),
            pltpu.VMEM((items, 2, rows, DH), low),
            pltpu.VMEM((items, 2, rows, DH), low),
            pltpu.VMEM((items, 2, rows, DH), low),
            pltpu.VMEM((micro, DH, DH), full),
            pltpu.VMEM((2, DH, DH), low),
            pltpu.VMEM(segments.shape, jnp.int32),
            dma(()),
            dma((items,)),
            dma((items, 2)),
            dma((items, 2)),
            dma((items, 2)),
            dma((chunks,)),
            dma((chunks,)),
            dma((items,)),
            dma((items,)),
            dma((chunks,)),
            dma((items, 2)),
        ],
        compiler_params=pltpu.CompilerParams(
            collective_id=0, has_side_effects=True, vmem_limit_bytes=60 * 1024 * 1024
        ),
        cost_estimate=pl.CostEstimate(
            flops=10 * items * group * rows * 2 * rows * DH,
            bytes_accessed=6 * 1024 * 1024,
            transcendentals=items * group * rows * rows,
        ),
    )(queries, keys, values, out_grad, segments)
    pieces = 4
    return pl.pallas_call(
        functools.partial(hand_over, pieces),
        out_shape=shapes,
        in_specs=[anywhere] * 3,
        out_specs=(anywhere,) * 3,
        scratch_shapes=[dma((3, pieces))],
        compiler_params=pltpu.CompilerParams(vmem_limit_bytes=60 * 1024 * 1024),
    )(*grads)


def solution(mesh):
    sizes = dict(mesh.shape)
    split = P("pipe", None, "seq", None)
    return jax.shard_map(
        functools.partial(per_device, sizes["pipe"], sizes["seq"]),
        mesh=mesh,
        in_specs=(split, split, split, P(None, "seq", None), P()),
        out_specs=(split, split, split),
        check_vma=False,
    )
```

```python
import functools

import jax
import jax.numpy as jnp
from jax import lax
from jax.experimental import pallas as pl
from jax.experimental.pallas import tpu as pltpu
from jax.sharding import PartitionSpec as P

DH = 128
LOG2E = 1.4426950408889634
MESH = pl.DeviceIdType.MESH

NT = (((1,), (1,)), ((), ()))
TN = (((0,), (0,)), ((), ()))
NN = (((1,), (0,)), ((), ()))


def dot(left, right, dims):
    return lax.dot_general(left, right, dims, preferred_element_type=jnp.float32)


def stack_heads(rows):
    count = rows.shape[1] // DH
    return jnp.concatenate([rows[:, i * DH : (i + 1) * DH] for i in range(count)], axis=0)


def loop(start, stop, body):
    def step(i, carry):
        body(i)
        return carry

    lax.fori_loop(start, stop, step, 0)


def kernel(
    sections,
    seq_size,
    kv_heads,
    group,
    q_hbm,
    k_hbm,
    v_hbm,
    g_hbm,
    seg_hbm,
    qg_hbm,
    kg_hbm,
    vg_hbm,
    x_buf,
    kv_buf,
    top_buf,
    prob_buf,
    ds_buf,
    g_in,
    g_out,
    qg_buf,
    part_own,
    part_send,
    part_recv,
    kv_out,
    bias_ref,
    pick_ref,
    seg_ref,
    seg_sem,
    x_sem,
    top_sem,
    own_sem,
    halo_send,
    halo_recv,
    g_send,
    g_recv,
    part_send_sem,
    part_recv_sem,
    qg_sem,
    kvg_sem,
):
    section = lax.axis_index("pipe")
    block = lax.axis_index("seq")
    micro = q_hbm.shape[1]
    items = micro * kv_heads
    scale = DH**-0.5
    last = section == sections - 1
    has_next = section > 0
    has_left = block > 0
    has_right = block < seq_size - 1
    edge = tuple((i, 1) for i in range(group))
    inner = tuple((i, 2) for i in range(0, group, 2)) if group % 2 == 0 else edge

    def place(item):
        head = lax.rem(item, kv_heads)
        return (
            item // kv_heads,
            pl.multiple_of(head * DH, DH),
            pl.multiple_of(head * group * DH, DH),
        )

    seg_copy = pltpu.make_async_copy(seg_hbm, seg_ref, seg_sem)

    def x_copy(b):
        return pltpu.make_async_copy(q_hbm.at[0, b], x_buf.at[b], x_sem.at[b])

    def top_copy(b):
        return pltpu.make_async_copy(g_hbm.at[b], top_buf.at[b], top_sem.at[b])

    def own_copies(b):
        return tuple(
            pltpu.make_async_copy(ref.at[0, b], kv_buf.at[i, b, 1], own_sem.at[i, b])
            for i, ref in enumerate((k_hbm, v_hbm))
        )

    def halo_copies(b, stage):
        width = kv_heads * DH
        cols = {0: pl.ds(0, DH), 1: pl.ds(DH, width - DH), 2: pl.ds(0, width)}[stage]
        at = b + 1 if stage == 2 else stage
        return tuple(
            pltpu.make_async_remote_copy(
                src_ref=ref.at[0, b, :, cols],
                dst_ref=kv_buf.at[i, b, 0, :, cols],
                send_sem=halo_send.at[i, at],
                recv_sem=halo_recv.at[i, at],
                device_id=(section, block + 1),
                device_id_type=MESH,
            )
            for i, ref in enumerate((k_hbm, v_hbm))
        )

    all_halos = [(0, 0)] + ([(0, 1)] if kv_heads > 1 else []) + [(b, 2) for b in range(1, micro)]

    def grad_copy(item, head, count):
        return pltpu.make_async_remote_copy(
            src_ref=g_out.at[item, pl.ds(head, count)],
            dst_ref=g_in.at[item, pl.ds(head, count)],
            send_sem=g_send,
            recv_sem=g_recv.at[item, head],
            device_id=(section - 1, block),
            device_id_type=MESH,
        )

    def part_copy(item):
        return pltpu.make_async_remote_copy(
            src_ref=part_send.at[item],
            dst_ref=part_recv.at[item],
            send_sem=part_send_sem,
            recv_sem=part_recv_sem,
            device_id=(section, block - 1),
            device_id_type=MESH,
        )

    barrier = pltpu.get_barrier_semaphore()
    neighbours = (
        (has_right, (section, block + 1)),
        (has_left, (section, block - 1)),
        (has_next, (section - 1, block)),
        (section < sections - 1, (section + 1, block)),
    )
    for exists, device in neighbours:

        @pl.when(exists)
        def _(device=device):
            pl.semaphore_signal(barrier, inc=1, device_id=device, device_id_type=MESH)

    seg_copy.start()
    for b in range(micro):
        for copy in own_copies(b):
            copy.start()
        x_copy(b).start()

        @pl.when(last)
        def _(b=b):
            top_copy(b).start()

    pl.semaphore_wait(barrier, sum(exists.astype(jnp.int32) for exists, _ in neighbours))

    @pl.when(has_right)
    def _():
        for b, stage in all_halos:
            for copy in halo_copies(b, stage):
                copy.start()

    @pl.when(jnp.logical_not(has_left))
    def _():
        for i in range(2):
            for b in range(micro):
                kv_buf[i, b, 0] = jnp.zeros(kv_buf.shape[3:], jnp.bfloat16)

    @pl.when(jnp.logical_not(has_right))
    def _():
        def clear(item):
            part_recv[item] = jnp.zeros(part_recv.shape[1:], jnp.bfloat16)

        loop(0, items, clear)

    key_at = lax.broadcasted_iota(jnp.int32, (DH, DH), 0)
    query_at = lax.broadcasted_iota(jnp.int32, (DH, DH), 1)
    in_own = key_at <= query_at
    before = jnp.maximum(block - 1, 0)
    seg_copy.wait()
    for b in range(micro):
        seg_query = seg_ref[b : b + 1, pl.ds(pl.multiple_of(block * DH, DH), DH)]
        seg_halo = seg_ref[b : b + 1, pl.ds(pl.multiple_of(before * DH, DH), DH)]
        seg_query = jnp.broadcast_to(seg_query.astype(jnp.float32), (DH, DH))
        seg_halo = jnp.broadcast_to(seg_halo.astype(jnp.float32), (DH, DH))
        seg_halo = jnp.where(has_left, seg_halo, -1.0)
        seg_key = jnp.where(in_own, seg_query.T, seg_halo.T)
        bias_ref[b] = jnp.where(seg_key == seg_query, 0.0, -1e30)
    pick_ref[0] = jnp.where(in_own, 0.0, 1.0).astype(jnp.bfloat16)
    pick_ref[1] = jnp.where(in_own, 1.0, 0.0).astype(jnp.bfloat16)

    def merge(both):
        count = both.shape[1] // DH
        keep = jnp.concatenate([in_own] * count, axis=1)
        return jnp.where(keep, both[DH:], both[:DH])

    def spread(packed):
        count = packed.shape[1] // DH
        return jnp.concatenate(
            [jnp.concatenate([pick_ref[i]] * count, axis=1) * packed for i in range(2)], axis=0
        )

    def rows_of(i, item):
        b, col, _ = place(item)
        return kv_buf[i, b, :, :, pl.ds(col, DH)].reshape(2 * DH, DH)

    def heads_of(ref, item, head, count):
        b, _, col = place(item)
        at = pl.multiple_of(col + head * DH, DH)
        return stack_heads(ref[b, :, pl.ds(at, count * DH)])

    def wait_halo(b, stage):
        @pl.when(has_left)
        def _():
            for copy in halo_copies(b, stage):
                copy.wait_recv()

    def wait_batch(b):
        for copy in own_copies(b):
            copy.wait()
        x_copy(b).wait()

        @pl.when(last)
        def _():
            top_copy(b).wait()

    def wait_first():
        wait_batch(0)
        wait_halo(0, 0)

    def wait_second():
        if kv_heads > 1:
            wait_halo(0, 1)

    def wait_later(b):
        wait_batch(b)
        wait_halo(b, 2)

    def probabilities(item, head, count):
        query = heads_of(x_buf, item, head, count)
        bias = jnp.concatenate([bias_ref[item // kv_heads]] * count, axis=1)
        score = merge(dot(rows_of(0, item), query, NT)) + bias
        top = jnp.max(score, axis=0, keepdims=True)
        weight = jnp.exp2((score - top) * (scale * LOG2E))
        total = jnp.sum(weight, axis=0, keepdims=True)
        prob_buf[item, :, head * DH : (head + count) * DH] = weight * (1.0 / total)

    def store_part(item, i, total):
        part_send[item, i] = total[:DH].astype(jnp.bfloat16)
        part_own[item, i] = total[DH:]

    def key_grad(item):
        query = heads_of(x_buf, item, 0, group)
        store_part(item, 0, dot(ds_buf[item], query, NN) * scale)

    def top_grad(item, head, count):
        return heads_of(top_buf, item, head, count)

    def sent_grad(item, head, count):
        return g_in[item, head : head + count].reshape(count * DH, DH)

    def value_grad(item, grad_of):
        grad = grad_of(item, 0, group)
        store_part(item, 1, dot(spread(prob_buf[item].astype(jnp.bfloat16)), grad, NN))

    def send_part(item):
        @pl.when(has_left)
        def _():
            part_copy(item).start()

    def both_grads(item, grad_of):
        key_grad(item)
        value_grad(item, grad_of)
        send_part(item)

    def backward(item, messages, grad_of, beside):
        b, _, wide_col = place(item)
        for head, count in messages:
            if grad_of is sent_grad:
                grad_copy(item, head, count).wait_recv()
            beside(head, count, True)
            cols = slice(head * DH, (head + count) * DH)
            key, value = rows_of(0, item), rows_of(1, item)
            grad = grad_of(item, head, count)
            prob = prob_buf[item, :, cols]
            prob_low = prob.astype(jnp.bfloat16)
            grad_prob = merge(dot(value, grad, NT))
            delta = jnp.sum(prob_low.astype(jnp.float32) * grad_prob, axis=0, keepdims=True)
            grad_score = spread((prob * (grad_prob - delta)).astype(jnp.bfloat16))
            query_grad = dot(grad_score, key, TN) * scale
            grad_next = (grad.astype(jnp.float32) + query_grad).astype(jnp.bfloat16)
            g_out[item, head : head + count] = grad_next.reshape(count, DH, DH)
            beside(head, count, False)
            ds_buf[item, :, cols] = grad_score

            @pl.when(has_next)
            def _():
                grad_copy(item, head, count).start()

            for i in range(count):
                at = pl.multiple_of(wide_col + (head + i) * DH, DH)
                qg_buf[b, :, pl.ds(at, DH)] = grad_next[i * DH : (i + 1) * DH]
        at = pl.ds(wide_col, group * DH)
        pltpu.make_async_copy(qg_buf.at[b, :, at], qg_hbm.at[0, b, :, at], qg_sem).start()

    def nothing(head, count, first):
        pass

    @pl.when(last)
    def _():
        wait_first()

        def at_once(head, count, first):
            if first:
                probabilities(0, head, count)

        backward(0, edge, top_grad, at_once)
        wait_second()
        probabilities(1, 0, group)

        def one(item):
            @pl.when(lax.rem(item + 1, kv_heads) == 0)
            def _():
                wait_later((item + 1) // kv_heads)

            def ahead(head, count, first):
                if not first:
                    probabilities(item + 1, head, count)

            backward(item, inner, top_grad, ahead)

        loop(1, items - 1, one)
        backward(items - 1, edge, top_grad, nothing)
        loop(0, items, lambda item: both_grads(item, top_grad))

    @pl.when(jnp.logical_not(last))
    def _():
        wait_first()
        wait_second()
        loop(0, kv_heads, lambda item: probabilities(item, 0, group))
        for b in range(1, micro):
            wait_later(b)
        loop(kv_heads, items, lambda item: probabilities(item, 0, group))
        backward(0, edge, sent_grad, nothing)

        def behind_of(i, half):
            def behind(head, count, first):
                if not first and head == 0:
                    key_grad(i)
                if not first and head == half:
                    value_grad(i, sent_grad)

            return behind

        def one(item):
            backward(item, inner, sent_grad, behind_of(item - 1, inner[-1][0]))
            send_part(item - 1)

        loop(1, items - 1, one)
        backward(items - 1, edge, sent_grad, behind_of(items - 2, 1))
        send_part(items - 2)
        both_grads(items - 1, sent_grad)

    @pl.when(has_right)
    def _():
        pltpu.make_async_copy(part_recv, part_recv, part_recv_sem).wait()

    def finish(item):
        b, col, _ = place(item)
        for i in range(2):
            total = part_own[item, i] + part_recv[item, i].astype(jnp.float32)
            kv_out[i, b, :, pl.ds(col, DH)] = total.astype(jnp.bfloat16)

    loop(0, items, finish)
    results = tuple(
        pltpu.make_async_copy(kv_out.at[i], ref.at[0], kvg_sem.at[i])
        for i, ref in enumerate((kg_hbm, vg_hbm))
    )
    for copy in results:
        copy.start()

    @pl.when(has_next)
    def _():
        pltpu.make_async_copy(g_out, g_out, g_send).wait()

    @pl.when(has_right)
    def _():
        for b, stage in all_halos:
            for copy in halo_copies(b, stage):
                copy.wait_send()

    @pl.when(has_left)
    def _():
        pltpu.make_async_copy(part_send, part_send, part_send_sem).wait()

    pltpu.make_async_copy(qg_buf, qg_hbm.at[0], qg_sem).wait()
    for copy in results:
        copy.wait()


def hand_over(*refs):
    count = len(refs) // 3
    sources, results, held = refs[:count], refs[count : 2 * count], refs[2 * count : 3 * count]
    sem = refs[3 * count]
    micro = sources[0].shape[1]
    takes, gives = [], []
    for i in range(count):
        for b in range(micro):
            at = (0, b)
            takes.append(pltpu.make_async_copy(sources[i].at[at], held[i].at[at], sem.at[0, i, b]))
            gives.append(pltpu.make_async_copy(held[i].at[at], results[i].at[at], sem.at[1, i, b]))
    for take in takes:
        take.start()
    for take, give in zip(takes, gives):
        take.wait()
        give.start()
    for give in gives:
        give.wait()


def per_device(sections, seq_size, queries, keys, values, out_grad, segments):
    micro, rows, query_width = queries.shape[1:]
    key_width = keys.shape[3]
    kv_heads = key_width // DH
    group = query_width // key_width
    items = micro * kv_heads
    anywhere = pl.BlockSpec(memory_space=pl.ANY)
    low, full = jnp.bfloat16, jnp.float32
    dma = pltpu.SemaphoreType.DMA
    shapes = tuple(jax.ShapeDtypeStruct(x.shape, low) for x in (queries, keys, values))
    grads = pl.pallas_call(
        functools.partial(kernel, sections, seq_size, kv_heads, group),
        out_shape=shapes,
        in_specs=[anywhere] * 5,
        out_specs=(anywhere,) * 3,
        scratch_shapes=[
            pltpu.VMEM((micro, rows, query_width), low),
            pltpu.VMEM((2, micro, 2, rows, key_width), low),
            pltpu.VMEM((micro, rows, query_width), low),
            pltpu.VMEM((items, rows, group * DH), full),
            pltpu.VMEM((items, 2 * rows, group * DH), low),
            pltpu.VMEM((items, group, rows, DH), low),
            pltpu.VMEM((items, group, rows, DH), low),
            pltpu.VMEM((micro, rows, query_width), low),
            pltpu.VMEM((items, 2, rows, DH), full),
            pltpu.VMEM((items, 2, rows, DH), low),
            pltpu.VMEM((items, 2, rows, DH), low),
            pltpu.VMEM((2, micro, rows, key_width), low),
            pltpu.VMEM((micro, DH, DH), full),
            pltpu.VMEM((2, DH, DH), low),
            pltpu.VMEM(segments.shape, jnp.int32),
            dma(()),
            dma((micro,)),
            dma((micro,)),
            dma((2, micro)),
            dma((2, micro + 1)),
            dma((2, micro + 1)),
            dma(()),
            dma((items, group)),
            dma(()),
            dma(()),
            dma(()),
            dma((2,)),
        ],
        compiler_params=pltpu.CompilerParams(
            collective_id=0, has_side_effects=True, vmem_limit_bytes=60 * 1024 * 1024
        ),
        cost_estimate=pl.CostEstimate(
            flops=10 * items * group * rows * 2 * rows * DH,
            bytes_accessed=6 * 1024 * 1024,
            transcendentals=items * group * rows * rows,
        ),
    )(queries, keys, values, out_grad, segments)
    return pl.pallas_call(
        hand_over,
        out_shape=shapes,
        in_specs=[anywhere] * 3,
        out_specs=(anywhere,) * 3,
        scratch_shapes=[pltpu.VMEM(x.shape, low) for x in shapes] + [dma((2, 3, micro))],
        compiler_params=pltpu.CompilerParams(vmem_limit_bytes=60 * 1024 * 1024),
    )(*grads)


def solution(mesh):
    sizes = dict(mesh.shape)
    split = P("pipe", None, "seq", None)
    return jax.shard_map(
        functools.partial(per_device, sizes["pipe"], sizes["seq"]),
        mesh=mesh,
        in_specs=(split, split, split, P(None, "seq", None), P()),
        out_specs=(split, split, split),
        check_vma=False,
    )
```

```python
import functools

import jax
import jax.numpy as jnp
from jax import lax
from jax.experimental import pallas as pl
from jax.experimental.pallas import tpu as pltpu
from jax.sharding import PartitionSpec as P

DH = 128
LOG2E = 1.4426950408889634
MESH = pl.DeviceIdType.MESH

NT = (((1,), (1,)), ((), ()))
NN = (((1,), (0,)), ((), ()))


def dot(left, right, dims):
    return lax.dot_general(left, right, dims, preferred_element_type=jnp.float32)


def stack_heads(rows):
    count = rows.shape[1] // DH
    return jnp.concatenate([rows[:, i * DH : (i + 1) * DH] for i in range(count)], axis=0)


def loop(start, stop, body):
    def step(i, carry):
        body(i)
        return carry

    lax.fori_loop(start, stop, step, 0)


def kernel(
    sections,
    seq_size,
    kv_heads,
    group,
    q_hbm,
    k_hbm,
    v_hbm,
    g_hbm,
    seg_hbm,
    qg_hbm,
    kg_hbm,
    vg_hbm,
    x_buf,
    kv_buf,
    top_buf,
    key_t,
    prob_buf,
    ds_buf,
    g_in,
    g_out,
    qg_buf,
    part_own,
    part_send,
    part_recv,
    kv_out,
    bias_ref,
    pick_ref,
    seg_ref,
    seg_sem,
    x_sem,
    top_sem,
    own_sem,
    halo_send,
    halo_recv,
    g_send,
    g_recv,
    part_send_sem,
    part_recv_sem,
    qg_sem,
    kvg_sem,
):
    section = lax.axis_index("pipe")
    block = lax.axis_index("seq")
    micro = q_hbm.shape[1]
    items = micro * kv_heads
    scale = DH**-0.5
    last = section == sections - 1
    has_next = section > 0
    has_left = block > 0
    has_right = block < seq_size - 1
    edge = tuple((i, 1) for i in range(group))
    inner = tuple((i, 2) for i in range(0, group, 2)) if group % 2 == 0 else edge

    def place(item):
        head = lax.rem(item, kv_heads)
        return (
            item // kv_heads,
            pl.multiple_of(head * DH, DH),
            pl.multiple_of(head * group * DH, DH),
        )

    seg_copy = pltpu.make_async_copy(seg_hbm, seg_ref, seg_sem)

    def x_copy(b):
        return pltpu.make_async_copy(q_hbm.at[0, b], x_buf.at[b], x_sem.at[b])

    def top_copy(b):
        return pltpu.make_async_copy(g_hbm.at[b], top_buf.at[b], top_sem.at[b])

    def own_copies(b):
        return tuple(
            pltpu.make_async_copy(ref.at[0, b], kv_buf.at[i, b, 1], own_sem.at[i, b])
            for i, ref in enumerate((k_hbm, v_hbm))
        )

    def halo_copies(b, stage):
        width = kv_heads * DH
        cols = {0: pl.ds(0, DH), 1: pl.ds(DH, width - DH), 2: pl.ds(0, width)}[stage]
        at = b + 1 if stage == 2 else stage
        return tuple(
            pltpu.make_async_remote_copy(
                src_ref=ref.at[0, b, :, cols],
                dst_ref=kv_buf.at[i, b, 0, :, cols],
                send_sem=halo_send.at[i, at],
                recv_sem=halo_recv.at[i, at],
                device_id=(section, block + 1),
                device_id_type=MESH,
            )
            for i, ref in enumerate((k_hbm, v_hbm))
        )

    all_halos = [(0, 0)] + ([(0, 1)] if kv_heads > 1 else []) + [(b, 2) for b in range(1, micro)]

    def grad_copy(item, head, count):
        return pltpu.make_async_remote_copy(
            src_ref=g_out.at[item, pl.ds(head, count)],
            dst_ref=g_in.at[item, pl.ds(head, count)],
            send_sem=g_send,
            recv_sem=g_recv.at[item, head],
            device_id=(section - 1, block),
            device_id_type=MESH,
        )

    def part_copy(item):
        return pltpu.make_async_remote_copy(
            src_ref=part_send.at[item],
            dst_ref=part_recv.at[item],
            send_sem=part_send_sem,
            recv_sem=part_recv_sem,
            device_id=(section, block - 1),
            device_id_type=MESH,
        )

    barrier = pltpu.get_barrier_semaphore()
    neighbours = (
        (has_right, (section, block + 1)),
        (has_left, (section, block - 1)),
        (has_next, (section - 1, block)),
        (section < sections - 1, (section + 1, block)),
    )
    for exists, device in neighbours:

        @pl.when(exists)
        def _(device=device):
            pl.semaphore_signal(barrier, inc=1, device_id=device, device_id_type=MESH)

    seg_copy.start()
    for b in range(micro):
        for copy in own_copies(b):
            copy.start()
        x_copy(b).start()

        @pl.when(last)
        def _(b=b):
            top_copy(b).start()

    pl.semaphore_wait(barrier, sum(exists.astype(jnp.int32) for exists, _ in neighbours))

    @pl.when(has_right)
    def _():
        for b, stage in all_halos:
            for copy in halo_copies(b, stage):
                copy.start()

    @pl.when(jnp.logical_not(has_left))
    def _():
        for i in range(2):
            for b in range(micro):
                kv_buf[i, b, 0] = jnp.zeros(kv_buf.shape[3:], jnp.bfloat16)

    @pl.when(jnp.logical_not(has_right))
    def _():
        def clear(item):
            part_recv[item] = jnp.zeros(part_recv.shape[1:], jnp.bfloat16)

        loop(0, items, clear)

    key_at = lax.broadcasted_iota(jnp.int32, (DH, DH), 0)
    query_at = lax.broadcasted_iota(jnp.int32, (DH, DH), 1)
    in_own = key_at <= query_at
    before = jnp.maximum(block - 1, 0)
    seg_copy.wait()
    for b in range(micro):
        seg_query = seg_ref[b : b + 1, pl.ds(pl.multiple_of(block * DH, DH), DH)]
        seg_halo = seg_ref[b : b + 1, pl.ds(pl.multiple_of(before * DH, DH), DH)]
        seg_query = jnp.broadcast_to(seg_query.astype(jnp.float32), (DH, DH))
        seg_halo = jnp.broadcast_to(seg_halo.astype(jnp.float32), (DH, DH))
        seg_halo = jnp.where(has_left, seg_halo, -1.0)
        seg_key = jnp.where(in_own, seg_query.T, seg_halo.T)
        bias_ref[b] = jnp.where(seg_key == seg_query, 0.0, -1e30)
    pick_ref[0] = jnp.where(in_own, 0.0, 1.0).astype(jnp.bfloat16)
    pick_ref[1] = jnp.where(in_own, 1.0, 0.0).astype(jnp.bfloat16)

    def merge(both):
        count = both.shape[1] // DH
        keep = jnp.concatenate([in_own] * count, axis=1)
        return jnp.where(keep, both[DH:], both[:DH])

    def spread(packed):
        count = packed.shape[1] // DH
        return jnp.concatenate(
            [jnp.concatenate([pick_ref[i]] * count, axis=1) * packed for i in range(2)], axis=0
        )

    def rows_of(i, item):
        b, col, _ = place(item)
        return kv_buf[i, b, :, :, pl.ds(col, DH)].reshape(2 * DH, DH)

    def heads_of(ref, item, head, count):
        b, _, col = place(item)
        at = pl.multiple_of(col + head * DH, DH)
        return stack_heads(ref[b, :, pl.ds(at, count * DH)])

    def wait_halo(b, stage):
        @pl.when(has_left)
        def _():
            for copy in halo_copies(b, stage):
                copy.wait_recv()

    def wait_batch(b):
        for copy in own_copies(b):
            copy.wait()
        x_copy(b).wait()

        @pl.when(last)
        def _():
            top_copy(b).wait()

    def wait_first():
        wait_batch(0)
        wait_halo(0, 0)

    def wait_second():
        if kv_heads > 1:
            wait_halo(0, 1)

    def wait_later(b):
        wait_batch(b)
        wait_halo(b, 2)

    def probabilities(item, head, count):
        if head == 0:
            key_t[item] = rows_of(0, item).T
        query = heads_of(x_buf, item, head, count)
        bias = jnp.concatenate([bias_ref[item // kv_heads]] * count, axis=1)
        score = merge(dot(rows_of(0, item), query, NT)) + bias
        top = jnp.max(score, axis=0, keepdims=True)
        weight = jnp.exp2((score - top) * (scale * LOG2E))
        total = jnp.sum(weight, axis=0, keepdims=True)
        prob_buf[item, :, head * DH : (head + count) * DH] = weight * (1.0 / total)

    def store_part(item, i, total):
        part_send[item, i] = total[:DH].astype(jnp.bfloat16)
        part_own[item, i] = total[DH:]

    def key_grad(item):
        query = heads_of(x_buf, item, 0, group)
        store_part(item, 0, dot(ds_buf[item], query, NN) * scale)

    def top_grad(item, head, count):
        rows = heads_of(top_buf, item, head, count)
        return jnp.concatenate([rows[i * DH : (i + 1) * DH].T for i in range(count)], axis=1)

    def sent_grad(item, head, count):
        return jnp.concatenate([g_in[item, head + i] for i in range(count)], axis=1)

    def value_grad(item, grad_of):
        prob_low = spread(prob_buf[item].astype(jnp.bfloat16))
        if grad_of is top_grad:
            total = dot(prob_low, heads_of(top_buf, item, 0, group), NN)
        else:
            total = dot(prob_low, grad_of(item, 0, group), NT)
        store_part(item, 1, total)

    def send_part(item):
        @pl.when(has_left)
        def _():
            part_copy(item).start()

    def both_grads(item, grad_of):
        key_grad(item)
        value_grad(item, grad_of)
        send_part(item)

    def backward(item, messages, grad_of, beside):
        b, _, wide_col = place(item)
        for head, count in messages:
            if grad_of is sent_grad:
                grad_copy(item, head, count).wait_recv()
            beside(head, count, True)
            cols = slice(head * DH, (head + count) * DH)
            value = rows_of(1, item)
            grad = grad_of(item, head, count)
            prob = prob_buf[item, :, cols]
            prob_low = prob.astype(jnp.bfloat16)
            grad_prob = merge(dot(value, grad, NN))
            delta = jnp.sum(prob_low.astype(jnp.float32) * grad_prob, axis=0, keepdims=True)
            grad_score = spread((prob * (grad_prob - delta)).astype(jnp.bfloat16))
            query_grad = dot(key_t[item], grad_score, NN) * scale
            grad_next = (grad.astype(jnp.float32) + query_grad).astype(jnp.bfloat16)
            for i in range(count):
                g_out[item, head + i] = grad_next[:, i * DH : (i + 1) * DH]
            beside(head, count, False)
            ds_buf[item, :, cols] = grad_score

            @pl.when(has_next)
            def _():
                grad_copy(item, head, count).start()

            for i in range(count):
                at = pl.multiple_of(wide_col + (head + i) * DH, DH)
                qg_buf[b, :, pl.ds(at, DH)] = grad_next[:, i * DH : (i + 1) * DH].T
        at = pl.ds(wide_col, group * DH)
        pltpu.make_async_copy(qg_buf.at[b, :, at], qg_hbm.at[0, b, :, at], qg_sem).start()

    def nothing(head, count, first):
        pass

    @pl.when(last)
    def _():
        wait_first()

        def at_once(head, count, first):
            if first:
                probabilities(0, head, count)

        backward(0, edge, top_grad, at_once)
        wait_second()
        probabilities(1, 0, group)

        def one(item):
            @pl.when(lax.rem(item + 1, kv_heads) == 0)
            def _():
                wait_later((item + 1) // kv_heads)

            def ahead(head, count, first):
                if not first:
                    probabilities(item + 1, head, count)

            backward(item, inner, top_grad, ahead)

        loop(1, items - 1, one)
        backward(items - 1, edge, top_grad, nothing)
        loop(0, items, lambda item: both_grads(item, top_grad))

    def behind_of(i, half):
        def behind(head, count, first):
            if not first and head == 0:
                key_grad(i)
            if not first and head == half:
                value_grad(i, sent_grad)

        return behind

    def one_sent(item):
        backward(item, inner, sent_grad, behind_of(item - 1, inner[-1][0]))
        send_part(item - 1)

    def last_sent():
        backward(items - 1, edge, sent_grad, behind_of(items - 2, 1))
        send_part(items - 2)
        both_grads(items - 1, sent_grad)

    @pl.when(section == sections - 2)
    def _():
        lead = kv_heads - 1
        wait_first()
        wait_second()
        loop(0, kv_heads, lambda item: probabilities(item, 0, group))
        backward(0, edge, sent_grad, nothing)
        for b in range(1, micro):
            wait_later(b)

        def both(item):
            behind = behind_of(item - 1, inner[-1][0])

            def beside(head, count, first):
                behind(head, count, first)
                if not first:
                    probabilities(item + lead, head, count)

            backward(item, inner, sent_grad, beside)
            send_part(item - 1)

        loop(1, items - lead, both)
        loop(items - lead, items - 1, one_sent)
        last_sent()

    @pl.when(section < sections - 2)
    def _():
        wait_first()
        wait_second()
        loop(0, kv_heads, lambda item: probabilities(item, 0, group))
        for b in range(1, micro):
            wait_later(b)
        loop(kv_heads, items, lambda item: probabilities(item, 0, group))
        backward(0, edge, sent_grad, nothing)
        loop(1, items - 1, one_sent)
        last_sent()

    @pl.when(has_right)
    def _():
        pltpu.make_async_copy(part_recv, part_recv, part_recv_sem).wait()

    def finish(item):
        b, col, _ = place(item)
        for i in range(2):
            total = part_own[item, i] + part_recv[item, i].astype(jnp.float32)
            kv_out[i, b, :, pl.ds(col, DH)] = total.astype(jnp.bfloat16)

    loop(0, items, finish)
    results = tuple(
        pltpu.make_async_copy(kv_out.at[i], ref.at[0], kvg_sem.at[i])
        for i, ref in enumerate((kg_hbm, vg_hbm))
    )
    for copy in results:
        copy.start()

    @pl.when(has_next)
    def _():
        pltpu.make_async_copy(g_out, g_out, g_send).wait()

    @pl.when(has_right)
    def _():
        for b, stage in all_halos:
            for copy in halo_copies(b, stage):
                copy.wait_send()

    @pl.when(has_left)
    def _():
        pltpu.make_async_copy(part_send, part_send, part_send_sem).wait()

    pltpu.make_async_copy(qg_buf, qg_hbm.at[0], qg_sem).wait()
    for copy in results:
        copy.wait()


def hand_over(*refs):
    count = len(refs) // 3
    sources, results, held = refs[:count], refs[count : 2 * count], refs[2 * count : 3 * count]
    sem = refs[3 * count]
    micro = sources[0].shape[1]
    takes, gives = [], []
    for i in range(count):
        for b in range(micro):
            at = (0, b)
            takes.append(pltpu.make_async_copy(sources[i].at[at], held[i].at[at], sem.at[0, i, b]))
            gives.append(pltpu.make_async_copy(held[i].at[at], results[i].at[at], sem.at[1, i, b]))
    for take in takes:
        take.start()
    for take, give in zip(takes, gives):
        take.wait()
        give.start()
    for give in gives:
        give.wait()


def per_device(sections, seq_size, queries, keys, values, out_grad, segments):
    micro, rows, query_width = queries.shape[1:]
    key_width = keys.shape[3]
    kv_heads = key_width // DH
    group = query_width // key_width
    items = micro * kv_heads
    anywhere = pl.BlockSpec(memory_space=pl.ANY)
    low, full = jnp.bfloat16, jnp.float32
    dma = pltpu.SemaphoreType.DMA
    shapes = tuple(jax.ShapeDtypeStruct(x.shape, low) for x in (queries, keys, values))
    grads = pl.pallas_call(
        functools.partial(kernel, sections, seq_size, kv_heads, group),
        out_shape=shapes,
        in_specs=[anywhere] * 5,
        out_specs=(anywhere,) * 3,
        scratch_shapes=[
            pltpu.VMEM((micro, rows, query_width), low),
            pltpu.VMEM((2, micro, 2, rows, key_width), low),
            pltpu.VMEM((micro, rows, query_width), low),
            pltpu.VMEM((items, DH, 2 * rows), low),
            pltpu.VMEM((items, rows, group * DH), full),
            pltpu.VMEM((items, 2 * rows, group * DH), low),
            pltpu.VMEM((items, group, rows, DH), low),
            pltpu.VMEM((items, group, rows, DH), low),
            pltpu.VMEM((micro, rows, query_width), low),
            pltpu.VMEM((items, 2, rows, DH), full),
            pltpu.VMEM((items, 2, rows, DH), low),
            pltpu.VMEM((items, 2, rows, DH), low),
            pltpu.VMEM((2, micro, rows, key_width), low),
            pltpu.VMEM((micro, DH, DH), full),
            pltpu.VMEM((2, DH, DH), low),
            pltpu.VMEM(segments.shape, jnp.int32),
            dma(()),
            dma((micro,)),
            dma((micro,)),
            dma((2, micro)),
            dma((2, micro + 1)),
            dma((2, micro + 1)),
            dma(()),
            dma((items, group)),
            dma(()),
            dma(()),
            dma(()),
            dma((2,)),
        ],
        compiler_params=pltpu.CompilerParams(
            collective_id=0, has_side_effects=True, vmem_limit_bytes=60 * 1024 * 1024
        ),
        cost_estimate=pl.CostEstimate(
            flops=10 * items * group * rows * 2 * rows * DH,
            bytes_accessed=6 * 1024 * 1024,
            transcendentals=items * group * rows * rows,
        ),
    )(queries, keys, values, out_grad, segments)
    return pl.pallas_call(
        hand_over,
        out_shape=shapes,
        in_specs=[anywhere] * 3,
        out_specs=(anywhere,) * 3,
        scratch_shapes=[pltpu.VMEM(x.shape, low) for x in shapes] + [dma((2, 3, micro))],
        compiler_params=pltpu.CompilerParams(vmem_limit_bytes=60 * 1024 * 1024),
    )(*grads)


def solution(mesh):
    sizes = dict(mesh.shape)
    split = P("pipe", None, "seq", None)
    return jax.shard_map(
        functools.partial(per_device, sizes["pipe"], sizes["seq"]),
        mesh=mesh,
        in_specs=(split, split, split, P(None, "seq", None), P()),
        out_specs=(split, split, split),
        check_vma=False,
    )
```

```python
import functools

import jax
import jax.numpy as jnp
from jax import lax
from jax.experimental import pallas as pl
from jax.experimental.pallas import tpu as pltpu
from jax.sharding import PartitionSpec as P

DH = 128
LOG2E = 1.4426950408889634
MESH = pl.DeviceIdType.MESH

NT = (((1,), (1,)), ((), ()))
NN = (((1,), (0,)), ((), ()))


def dot(left, right, dims):
    return lax.dot_general(left, right, dims, preferred_element_type=jnp.float32)


def stack_heads(rows):
    count = rows.shape[1] // DH
    return jnp.concatenate([rows[:, i * DH : (i + 1) * DH] for i in range(count)], axis=0)


def loop(start, stop, body):
    def step(i, carry):
        body(i)
        return carry

    lax.fori_loop(start, stop, step, 0)


def kernel(
    sections,
    seq_size,
    kv_heads,
    group,
    q_hbm,
    k_hbm,
    v_hbm,
    g_hbm,
    seg_hbm,
    qg_hbm,
    kg_hbm,
    vg_hbm,
    x_buf,
    kv_buf,
    top_buf,
    key_t,
    prob_buf,
    ds_buf,
    g_in,
    g_out,
    qg_buf,
    part_own,
    part_send,
    part_recv,
    kv_out,
    bias_ref,
    pick_ref,
    seg_ref,
    seg_sem,
    x_sem,
    top_sem,
    own_sem,
    halo_send,
    halo_recv,
    g_send,
    g_recv,
    part_send_sem,
    part_recv_sem,
    qg_sem,
    kvg_sem,
):
    section = lax.axis_index("pipe")
    block = lax.axis_index("seq")
    micro = q_hbm.shape[1]
    items = micro * kv_heads
    scale = DH**-0.5
    last = section == sections - 1
    has_next = section > 0
    has_left = block > 0
    has_right = block < seq_size - 1
    edge = tuple((i, 1) for i in range(group))
    inner = tuple((i, 2) for i in range(0, group, 2)) if group % 2 == 0 else edge

    def place(item):
        head = lax.rem(item, kv_heads)
        return (
            item // kv_heads,
            pl.multiple_of(head * DH, DH),
            pl.multiple_of(head * group * DH, DH),
        )

    seg_copy = pltpu.make_async_copy(seg_hbm, seg_ref, seg_sem)

    def x_copy(b):
        return pltpu.make_async_copy(q_hbm.at[0, b], x_buf.at[b], x_sem.at[b])

    def top_copy(b):
        return pltpu.make_async_copy(g_hbm.at[b], top_buf.at[b], top_sem.at[b])

    def own_copies(b):
        return tuple(
            pltpu.make_async_copy(ref.at[0, b], kv_buf.at[i, b, 1], own_sem.at[i, b])
            for i, ref in enumerate((k_hbm, v_hbm))
        )

    def halo_copies(b, stage):
        width = kv_heads * DH
        cols = {0: pl.ds(0, DH), 1: pl.ds(DH, width - DH), 2: pl.ds(0, width)}[stage]
        at = b + 1 if stage == 2 else stage
        return tuple(
            pltpu.make_async_remote_copy(
                src_ref=ref.at[0, b, :, cols],
                dst_ref=kv_buf.at[i, b, 0, :, cols],
                send_sem=halo_send.at[i, at],
                recv_sem=halo_recv.at[i, at],
                device_id=(section, block + 1),
                device_id_type=MESH,
            )
            for i, ref in enumerate((k_hbm, v_hbm))
        )

    all_halos = [(0, 0)] + ([(0, 1)] if kv_heads > 1 else []) + [(b, 2) for b in range(1, micro)]

    def grad_copy(item, head):
        return pltpu.make_async_remote_copy(
            src_ref=g_out.at[item, head],
            dst_ref=g_in.at[item, head],
            send_sem=g_send,
            recv_sem=g_recv.at[item, head],
            device_id=(section - 1, block),
            device_id_type=MESH,
        )

    def part_copy(item):
        return pltpu.make_async_remote_copy(
            src_ref=part_send.at[item],
            dst_ref=part_recv.at[item],
            send_sem=part_send_sem,
            recv_sem=part_recv_sem.at[item],
            device_id=(section, block - 1),
            device_id_type=MESH,
        )

    barrier = pltpu.get_barrier_semaphore()
    neighbours = (
        (has_right, (section, block + 1)),
        (has_left, (section, block - 1)),
        (has_next, (section - 1, block)),
        (section < sections - 1, (section + 1, block)),
    )
    for exists, device in neighbours:

        @pl.when(exists)
        def _(device=device):
            pl.semaphore_signal(barrier, inc=1, device_id=device, device_id_type=MESH)

    seg_copy.start()
    for b in range(micro):
        for copy in own_copies(b):
            copy.start()
        x_copy(b).start()

        @pl.when(last)
        def _(b=b):
            top_copy(b).start()

    pl.semaphore_wait(barrier, sum(exists.astype(jnp.int32) for exists, _ in neighbours))

    @pl.when(has_right)
    def _():
        for b, stage in all_halos:
            for copy in halo_copies(b, stage):
                copy.start()

    @pl.when(jnp.logical_not(has_left))
    def _():
        for i in range(2):
            for b in range(micro):
                kv_buf[i, b, 0] = jnp.zeros(kv_buf.shape[3:], jnp.bfloat16)

    @pl.when(jnp.logical_not(has_right))
    def _():
        def clear(item):
            part_recv[item] = jnp.zeros(part_recv.shape[1:], jnp.bfloat16)

        loop(0, items, clear)

    key_at = lax.broadcasted_iota(jnp.int32, (DH, DH), 0)
    query_at = lax.broadcasted_iota(jnp.int32, (DH, DH), 1)
    in_own = key_at <= query_at
    before = jnp.maximum(block - 1, 0)
    seg_copy.wait()
    for b in range(micro):
        seg_query = seg_ref[b : b + 1, pl.ds(pl.multiple_of(block * DH, DH), DH)]
        seg_halo = seg_ref[b : b + 1, pl.ds(pl.multiple_of(before * DH, DH), DH)]
        seg_query = jnp.broadcast_to(seg_query.astype(jnp.float32), (DH, DH))
        seg_halo = jnp.broadcast_to(seg_halo.astype(jnp.float32), (DH, DH))
        seg_halo = jnp.where(has_left, seg_halo, -1.0)
        seg_key = jnp.where(in_own, seg_query.T, seg_halo.T)
        bias_ref[b] = jnp.where(seg_key == seg_query, 0.0, -1e30)
    pick_ref[0] = jnp.where(in_own, 0.0, 1.0).astype(jnp.bfloat16)
    pick_ref[1] = jnp.where(in_own, 1.0, 0.0).astype(jnp.bfloat16)

    def merge(both):
        count = both.shape[1] // DH
        keep = jnp.concatenate([in_own] * count, axis=1)
        return jnp.where(keep, both[DH:], both[:DH])

    def spread(packed):
        count = packed.shape[1] // DH
        return jnp.concatenate(
            [jnp.concatenate([pick_ref[i]] * count, axis=1) * packed for i in range(2)], axis=0
        )

    def rows_of(i, item):
        b, col, _ = place(item)
        return kv_buf[i, b, :, :, pl.ds(col, DH)].reshape(2 * DH, DH)

    def heads_of(ref, item, head, count):
        b, _, col = place(item)
        at = pl.multiple_of(col + head * DH, DH)
        return stack_heads(ref[b, :, pl.ds(at, count * DH)])

    def wait_halo(b, stage):
        @pl.when(has_left)
        def _():
            for copy in halo_copies(b, stage):
                copy.wait_recv()

    def wait_batch(b):
        for copy in own_copies(b):
            copy.wait()
        x_copy(b).wait()

        @pl.when(last)
        def _():
            top_copy(b).wait()

    def wait_first():
        wait_batch(0)
        wait_halo(0, 0)

    def wait_second():
        if kv_heads > 1:
            wait_halo(0, 1)

    def wait_later(b):
        wait_batch(b)
        wait_halo(b, 2)

    def probabilities(item, head, count):
        if head == 0:
            key_t[item] = rows_of(0, item).T
        query = heads_of(x_buf, item, head, count)
        bias = jnp.concatenate([bias_ref[item // kv_heads]] * count, axis=1)
        score = merge(dot(rows_of(0, item), query, NT)) + bias
        top = jnp.max(score, axis=0, keepdims=True)
        weight = jnp.exp2((score - top) * (scale * LOG2E))
        total = jnp.sum(weight, axis=0, keepdims=True)
        prob_buf[item, :, head * DH : (head + count) * DH] = weight * (1.0 / total)

    def store_part(item, i, total):
        part_send[item, i] = total[:DH].astype(jnp.bfloat16)
        part_own[item, i] = total[DH:]

    def key_grad(item):
        query = heads_of(x_buf, item, 0, group)
        store_part(item, 0, dot(ds_buf[item], query, NN) * scale)

    def top_grad(item, head, count):
        rows = heads_of(top_buf, item, head, count)
        return jnp.concatenate([rows[i * DH : (i + 1) * DH].T for i in range(count)], axis=1)

    def sent_grad(item, head, count):
        return jnp.concatenate([g_in[item, head + i] for i in range(count)], axis=1)

    def value_grad(item, grad_of):
        prob_low = spread(prob_buf[item].astype(jnp.bfloat16))
        if grad_of is top_grad:
            total = dot(prob_low, heads_of(top_buf, item, 0, group), NN)
        else:
            total = dot(prob_low, grad_of(item, 0, group), NT)
        store_part(item, 1, total)

    def send_part(item):
        @pl.when(has_left)
        def _():
            part_copy(item).start()

    def both_grads(item, grad_of):
        key_grad(item)
        value_grad(item, grad_of)
        send_part(item)

    def backward(item, messages, grad_of, beside):
        b, _, wide_col = place(item)
        for head, count in messages:
            if grad_of is sent_grad:
                for i in range(count):
                    grad_copy(item, head + i).wait_recv()
            beside(head, count, True)
            cols = slice(head * DH, (head + count) * DH)
            value = rows_of(1, item)
            grad = grad_of(item, head, count)
            prob = prob_buf[item, :, cols]
            prob_low = prob.astype(jnp.bfloat16)
            grad_prob = merge(dot(value, grad, NN))
            delta = jnp.sum(prob_low.astype(jnp.float32) * grad_prob, axis=0, keepdims=True)
            grad_score = spread((prob * (grad_prob - delta)).astype(jnp.bfloat16))
            query_grad = dot(key_t[item], grad_score, NN) * scale
            grad_next = (grad.astype(jnp.float32) + query_grad).astype(jnp.bfloat16)
            for i in range(count):
                g_out[item, head + i] = grad_next[:, i * DH : (i + 1) * DH]
            beside(head, count, False)
            ds_buf[item, :, cols] = grad_score

            @pl.when(has_next)
            def _():
                for i in range(count):
                    grad_copy(item, head + i).start()

            for i in range(count):
                at = pl.multiple_of(wide_col + (head + i) * DH, DH)
                qg_buf[b, :, pl.ds(at, DH)] = grad_next[:, i * DH : (i + 1) * DH].T
        at = pl.ds(wide_col, group * DH)
        pltpu.make_async_copy(qg_buf.at[b, :, at], qg_hbm.at[0, b, :, at], qg_sem).start()

    def nothing(head, count, first):
        pass

    @pl.when(last)
    def _():
        wait_first()

        def at_once(head, count, first):
            if first:
                probabilities(0, head, count)

        backward(0, edge, top_grad, at_once)
        wait_second()
        probabilities(1, 0, group)

        def one(item):
            @pl.when(lax.rem(item + 1, kv_heads) == 0)
            def _():
                wait_later((item + 1) // kv_heads)

            def ahead(head, count, first):
                if not first:
                    probabilities(item + 1, head, count)

            backward(item, inner, top_grad, ahead)

        loop(1, items - 1, one)
        backward(items - 1, edge, top_grad, nothing)
        loop(0, items, lambda item: both_grads(item, top_grad))

    def behind_of(i, half):
        def behind(head, count, first):
            if not first and head == 0:
                key_grad(i)
            if not first and head == half:
                value_grad(i, sent_grad)

        return behind

    def one_sent(item):
        backward(item, edge, sent_grad, behind_of(item - 1, group // 2))
        send_part(item - 1)

    def last_sent():
        backward(items - 1, edge, sent_grad, behind_of(items - 2, 1))
        send_part(items - 2)
        both_grads(items - 1, sent_grad)

    @pl.when(section == sections - 2)
    def _():
        lead = kv_heads - 1
        wait_first()
        wait_second()
        loop(0, kv_heads, lambda item: probabilities(item, 0, group))
        backward(0, edge, sent_grad, nothing)
        for b in range(1, micro):
            wait_later(b)

        def both(item):
            behind = behind_of(item - 1, group // 2)

            def beside(head, count, first):
                behind(head, count, first)
                if not first:
                    probabilities(item + lead, head, count)

            backward(item, edge, sent_grad, beside)
            send_part(item - 1)

        loop(1, items - lead, both)
        loop(items - lead, items - 1, one_sent)
        last_sent()

    @pl.when(section < sections - 2)
    def _():
        wait_first()
        wait_second()
        loop(0, kv_heads, lambda item: probabilities(item, 0, group))
        for b in range(1, micro):
            wait_later(b)
        loop(kv_heads, items, lambda item: probabilities(item, 0, group))
        backward(0, edge, sent_grad, nothing)
        loop(1, items - 1, one_sent)
        last_sent()

    def finish(item):
        @pl.when(has_right)
        def _():
            part_copy(item).wait_recv()

        b, col, _ = place(item)
        for i in range(2):
            total = part_own[item, i] + part_recv[item, i].astype(jnp.float32)
            kv_out[i, b, :, pl.ds(col, DH)] = total.astype(jnp.bfloat16)

    loop(0, items, finish)
    results = tuple(
        pltpu.make_async_copy(kv_out.at[i], ref.at[0], kvg_sem.at[i])
        for i, ref in enumerate((kg_hbm, vg_hbm))
    )
    for copy in results:
        copy.start()

    @pl.when(has_next)
    def _():
        pltpu.make_async_copy(g_out, g_out, g_send).wait()

    @pl.when(has_right)
    def _():
        for b, stage in all_halos:
            for copy in halo_copies(b, stage):
                copy.wait_send()

    @pl.when(has_left)
    def _():
        pltpu.make_async_copy(part_send, part_send, part_send_sem).wait()

    pltpu.make_async_copy(qg_buf, qg_hbm.at[0], qg_sem).wait()
    for copy in results:
        copy.wait()


def hand_over(*refs):
    count = len(refs) // 3
    sources, results, held = refs[:count], refs[count : 2 * count], refs[2 * count : 3 * count]
    sem = refs[3 * count]
    micro = sources[0].shape[1]
    takes, gives = [], []
    for i in range(count):
        for b in range(micro):
            at = (0, b)
            takes.append(pltpu.make_async_copy(sources[i].at[at], held[i].at[at], sem.at[0, i, b]))
            gives.append(pltpu.make_async_copy(held[i].at[at], results[i].at[at], sem.at[1, i, b]))
    for take in takes:
        take.start()
    for take, give in zip(takes, gives):
        take.wait()
        give.start()
    for give in gives:
        give.wait()


def per_device(sections, seq_size, queries, keys, values, out_grad, segments):
    micro, rows, query_width = queries.shape[1:]
    key_width = keys.shape[3]
    kv_heads = key_width // DH
    group = query_width // key_width
    items = micro * kv_heads
    anywhere = pl.BlockSpec(memory_space=pl.ANY)
    low, full = jnp.bfloat16, jnp.float32
    dma = pltpu.SemaphoreType.DMA
    shapes = tuple(jax.ShapeDtypeStruct(x.shape, low) for x in (queries, keys, values))
    grads = pl.pallas_call(
        functools.partial(kernel, sections, seq_size, kv_heads, group),
        out_shape=shapes,
        in_specs=[anywhere] * 5,
        out_specs=(anywhere,) * 3,
        scratch_shapes=[
            pltpu.VMEM((micro, rows, query_width), low),
            pltpu.VMEM((2, micro, 2, rows, key_width), low),
            pltpu.VMEM((micro, rows, query_width), low),
            pltpu.VMEM((items, DH, 2 * rows), low),
            pltpu.VMEM((items, rows, group * DH), full),
            pltpu.VMEM((items, 2 * rows, group * DH), low),
            pltpu.VMEM((items, group, rows, DH), low),
            pltpu.VMEM((items, group, rows, DH), low),
            pltpu.VMEM((micro, rows, query_width), low),
            pltpu.VMEM((items, 2, rows, DH), full),
            pltpu.VMEM((items, 2, rows, DH), low),
            pltpu.VMEM((items, 2, rows, DH), low),
            pltpu.VMEM((2, micro, rows, key_width), low),
            pltpu.VMEM((micro, DH, DH), full),
            pltpu.VMEM((2, DH, DH), low),
            pltpu.VMEM(segments.shape, jnp.int32),
            dma(()),
            dma((micro,)),
            dma((micro,)),
            dma((2, micro)),
            dma((2, micro + 1)),
            dma((2, micro + 1)),
            dma(()),
            dma((items, group)),
            dma(()),
            dma((items,)),
            dma(()),
            dma((2,)),
        ],
        compiler_params=pltpu.CompilerParams(
            collective_id=0, has_side_effects=True, vmem_limit_bytes=60 * 1024 * 1024
        ),
        cost_estimate=pl.CostEstimate(
            flops=10 * items * group * rows * 2 * rows * DH,
            bytes_accessed=6 * 1024 * 1024,
            transcendentals=items * group * rows * rows,
        ),
    )(queries, keys, values, out_grad, segments)
    return pl.pallas_call(
        hand_over,
        out_shape=shapes,
        in_specs=[anywhere] * 3,
        out_specs=(anywhere,) * 3,
        scratch_shapes=[pltpu.VMEM(x.shape, low) for x in shapes] + [dma((2, 3, micro))],
        compiler_params=pltpu.CompilerParams(vmem_limit_bytes=60 * 1024 * 1024),
    )(*grads)


def solution(mesh):
    sizes = dict(mesh.shape)
    split = P("pipe", None, "seq", None)
    return jax.shard_map(
        functools.partial(per_device, sizes["pipe"], sizes["seq"]),
        mesh=mesh,
        in_specs=(split, split, split, P(None, "seq", None), P()),
        out_specs=(split, split, split),
        check_vma=False,
    )
```

```python
import functools

import jax
import jax.numpy as jnp
from jax import lax
from jax.experimental import pallas as pl
from jax.experimental.pallas import tpu as pltpu
from jax.sharding import PartitionSpec as P

DH = 128
LOG2E = 1.4426950408889634
MESH = pl.DeviceIdType.MESH

NT = (((1,), (1,)), ((), ()))
NN = (((1,), (0,)), ((), ()))


def dot(left, right, dims):
    return lax.dot_general(left, right, dims, preferred_element_type=jnp.float32)


def stack_heads(rows):
    count = rows.shape[1] // DH
    return jnp.concatenate([rows[:, i * DH : (i + 1) * DH] for i in range(count)], axis=0)


def loop(start, stop, body):
    def step(i, carry):
        body(i)
        return carry

    lax.fori_loop(start, stop, step, 0)


def kernel(
    sections,
    seq_size,
    kv_heads,
    group,
    q_hbm,
    k_hbm,
    v_hbm,
    g_hbm,
    seg_hbm,
    qg_hbm,
    kg_hbm,
    vg_hbm,
    x_buf,
    kv_buf,
    top_buf,
    key_t,
    prob_buf,
    ds_buf,
    g_in,
    g_out,
    qg_buf,
    part_own,
    part_send,
    part_recv,
    kv_out,
    bias_ref,
    pick_ref,
    seg_ref,
    seg_sem,
    x_sem,
    top_sem,
    own_sem,
    halo_send,
    halo_recv,
    g_send,
    g_recv,
    part_send_sem,
    part_recv_sem,
    qg_sem,
    kvg_sem,
):
    section = lax.axis_index("pipe")
    block = lax.axis_index("seq")
    micro = q_hbm.shape[1]
    items = micro * kv_heads
    scale = DH**-0.5
    last = section == sections - 1
    has_next = section > 0
    has_left = block > 0
    has_right = block < seq_size - 1
    edge = tuple((i, 1) for i in range(group))
    inner = tuple((i, 2) for i in range(0, group, 2)) if group % 2 == 0 else edge

    def place(item):
        head = lax.rem(item, kv_heads)
        return (
            item // kv_heads,
            pl.multiple_of(head * DH, DH),
            pl.multiple_of(head * group * DH, DH),
        )

    seg_copy = pltpu.make_async_copy(seg_hbm, seg_ref, seg_sem)

    def x_copy(b):
        return pltpu.make_async_copy(q_hbm.at[0, b], x_buf.at[b], x_sem.at[b])

    def top_copy(b):
        return pltpu.make_async_copy(g_hbm.at[b], top_buf.at[b], top_sem.at[b])

    def own_copies(b):
        return tuple(
            pltpu.make_async_copy(ref.at[0, b], kv_buf.at[i, b, 1], own_sem.at[i, b])
            for i, ref in enumerate((k_hbm, v_hbm))
        )

    def halo_copies(b, stage):
        width = kv_heads * DH
        cols = {0: pl.ds(0, DH), 1: pl.ds(DH, width - DH), 2: pl.ds(0, width)}[stage]
        at = b + 1 if stage == 2 else stage
        return tuple(
            pltpu.make_async_remote_copy(
                src_ref=ref.at[0, b, :, cols],
                dst_ref=kv_buf.at[i, b, 0, :, cols],
                send_sem=halo_send.at[i, at],
                recv_sem=halo_recv.at[i, at],
                device_id=(section, block + 1),
                device_id_type=MESH,
            )
            for i, ref in enumerate((k_hbm, v_hbm))
        )

    all_halos = [(0, 0)] + ([(0, 1)] if kv_heads > 1 else []) + [(b, 2) for b in range(1, micro)]

    def grad_copy(item, head):
        return pltpu.make_async_remote_copy(
            src_ref=g_out.at[item, head],
            dst_ref=g_in.at[item, head],
            send_sem=g_send,
            recv_sem=g_recv.at[item, head],
            device_id=(section - 1, block),
            device_id_type=MESH,
        )

    def part_copy(item):
        return pltpu.make_async_remote_copy(
            src_ref=part_send.at[item],
            dst_ref=part_recv.at[item],
            send_sem=part_send_sem,
            recv_sem=part_recv_sem.at[item],
            device_id=(section, block - 1),
            device_id_type=MESH,
        )

    barrier = pltpu.get_barrier_semaphore()
    neighbours = (
        (has_right, (section, block + 1)),
        (has_left, (section, block - 1)),
        (has_next, (section - 1, block)),
        (section < sections - 1, (section + 1, block)),
    )
    for exists, device in neighbours:

        @pl.when(exists)
        def _(device=device):
            pl.semaphore_signal(barrier, inc=1, device_id=device, device_id_type=MESH)

    seg_copy.start()
    for b in range(micro):
        for copy in own_copies(b):
            copy.start()
        x_copy(b).start()

        @pl.when(last)
        def _(b=b):
            top_copy(b).start()

    pl.semaphore_wait(barrier, sum(exists.astype(jnp.int32) for exists, _ in neighbours))

    @pl.when(has_right)
    def _():
        for b, stage in all_halos:
            for copy in halo_copies(b, stage):
                copy.start()

    @pl.when(jnp.logical_not(has_left))
    def _():
        for i in range(2):
            for b in range(micro):
                kv_buf[i, b, 0] = jnp.zeros(kv_buf.shape[3:], jnp.bfloat16)

    @pl.when(jnp.logical_not(has_right))
    def _():
        def clear(item):
            part_recv[item] = jnp.zeros(part_recv.shape[1:], jnp.bfloat16)

        loop(0, items, clear)

    key_at = lax.broadcasted_iota(jnp.int32, (DH, DH), 0)
    query_at = lax.broadcasted_iota(jnp.int32, (DH, DH), 1)
    in_own = key_at <= query_at
    before = jnp.maximum(block - 1, 0)
    seg_copy.wait()
    for b in range(micro):
        seg_query = seg_ref[b : b + 1, pl.ds(pl.multiple_of(block * DH, DH), DH)]
        seg_halo = seg_ref[b : b + 1, pl.ds(pl.multiple_of(before * DH, DH), DH)]
        seg_query = jnp.broadcast_to(seg_query.astype(jnp.float32), (DH, DH))
        seg_halo = jnp.broadcast_to(seg_halo.astype(jnp.float32), (DH, DH))
        seg_halo = jnp.where(has_left, seg_halo, -1.0)
        seg_key = jnp.where(in_own, seg_query.T, seg_halo.T)
        bias_ref[b] = jnp.where(seg_key == seg_query, 0.0, -1e30)
    pick_ref[0] = jnp.where(in_own, 0.0, 1.0).astype(jnp.bfloat16)
    pick_ref[1] = jnp.where(in_own, 1.0, 0.0).astype(jnp.bfloat16)

    def merge(both):
        count = both.shape[1] // DH
        keep = jnp.concatenate([in_own] * count, axis=1)
        return jnp.where(keep, both[DH:], both[:DH])

    def spread(packed):
        count = packed.shape[1] // DH
        return jnp.concatenate(
            [jnp.concatenate([pick_ref[i]] * count, axis=1) * packed for i in range(2)], axis=0
        )

    def rows_of(i, item):
        b, col, _ = place(item)
        return kv_buf[i, b, :, :, pl.ds(col, DH)].reshape(2 * DH, DH)

    def heads_of(ref, item, head, count):
        b, _, col = place(item)
        at = pl.multiple_of(col + head * DH, DH)
        return stack_heads(ref[b, :, pl.ds(at, count * DH)])

    def wait_halo(b, stage):
        @pl.when(has_left)
        def _():
            for copy in halo_copies(b, stage):
                copy.wait_recv()

    def wait_batch(b):
        for copy in own_copies(b):
            copy.wait()
        x_copy(b).wait()

        @pl.when(last)
        def _():
            top_copy(b).wait()

    def wait_first():
        wait_batch(0)
        wait_halo(0, 0)

    def wait_second():
        if kv_heads > 1:
            wait_halo(0, 1)

    def wait_later(b):
        wait_batch(b)
        wait_halo(b, 2)

    def probabilities(item, head, count):
        if head == 0:
            key_t[item] = rows_of(0, item).T
        query = heads_of(x_buf, item, head, count)
        bias = jnp.concatenate([bias_ref[item // kv_heads]] * count, axis=1)
        score = merge(dot(rows_of(0, item), query, NT)) + bias
        top = jnp.max(score, axis=0, keepdims=True)
        weight = jnp.exp2((score - top) * (scale * LOG2E))
        total = jnp.sum(weight, axis=0, keepdims=True)
        prob_buf[item, :, head * DH : (head + count) * DH] = weight * (1.0 / total)

    def store_part(item, i, total):
        part_send[item, i] = total[:DH].astype(jnp.bfloat16)
        part_own[item, i] = total[DH:]

    def key_grad(item):
        query = heads_of(x_buf, item, 0, group)
        store_part(item, 0, dot(ds_buf[item], query, NN) * scale)

    def top_grad(item, head, count):
        rows = heads_of(top_buf, item, head, count)
        return jnp.concatenate([rows[i * DH : (i + 1) * DH].T for i in range(count)], axis=1)

    def sent_grad(item, head, count):
        return jnp.concatenate([g_in[item, head + i] for i in range(count)], axis=1)

    def value_grad(item, grad_of):
        prob_low = spread(prob_buf[item].astype(jnp.bfloat16))
        if grad_of is top_grad:
            total = dot(prob_low, heads_of(top_buf, item, 0, group), NN)
        else:
            total = dot(prob_low, grad_of(item, 0, group), NT)
        store_part(item, 1, total)

    def send_part(item):
        @pl.when(has_left)
        def _():
            part_copy(item).start()

    def both_grads(item, grad_of):
        key_grad(item)
        value_grad(item, grad_of)
        send_part(item)

    def backward(item, messages, grad_of, beside):
        b, _, wide_col = place(item)
        for head, count in messages:
            if grad_of is sent_grad:
                for i in range(count):
                    grad_copy(item, head + i).wait_recv()
            beside(head, count, True)
            cols = slice(head * DH, (head + count) * DH)
            value = rows_of(1, item)
            grad = grad_of(item, head, count)
            prob = prob_buf[item, :, cols]
            prob_low = prob.astype(jnp.bfloat16)
            grad_prob = merge(dot(value, grad, NN))
            delta = jnp.sum(prob_low.astype(jnp.float32) * grad_prob, axis=0, keepdims=True)
            grad_score = spread((prob * (grad_prob - delta)).astype(jnp.bfloat16))
            query_grad = dot(key_t[item], grad_score, NN) * scale
            grad_next = (grad.astype(jnp.float32) + query_grad).astype(jnp.bfloat16)
            for i in range(count):
                g_out[item, head + i] = grad_next[:, i * DH : (i + 1) * DH]
            beside(head, count, False)
            ds_buf[item, :, cols] = grad_score

            @pl.when(has_next)
            def _():
                for i in range(count):
                    grad_copy(item, head + i).start()

            for i in range(count):
                at = pl.multiple_of(wide_col + (head + i) * DH, DH)
                qg_buf[b, :, pl.ds(at, DH)] = grad_next[:, i * DH : (i + 1) * DH].T
        at = pl.ds(wide_col, group * DH)
        pltpu.make_async_copy(qg_buf.at[b, :, at], qg_hbm.at[0, b, :, at], qg_sem).start()

    def nothing(head, count, first):
        pass

    @pl.when(last)
    def _():
        wait_first()

        def at_once(head, count, first):
            if first:
                probabilities(0, head, count)

        backward(0, edge, top_grad, at_once)
        wait_second()
        probabilities(1, 0, group)

        def one(item):
            @pl.when(lax.rem(item + 1, kv_heads) == 0)
            def _():
                wait_later((item + 1) // kv_heads)

            def ahead(head, count, first):
                if not first:
                    probabilities(item + 1, head, count)

            backward(item, inner, top_grad, ahead)

        loop(1, items - 1, one)
        backward(items - 1, edge, top_grad, nothing)
        loop(0, items, lambda item: both_grads(item, top_grad))

    def behind_of(i, half):
        def behind(head, count, first):
            if not first and head == 0:
                key_grad(i)
            if not first and head == half:
                value_grad(i, sent_grad)

        return behind

    def one_sent(item):
        backward(item, edge, sent_grad, behind_of(item - 1, group // 2))
        send_part(item - 1)

    def last_sent():
        behind = behind_of(items - 2, 0)

        def beside(head, count, first):
            behind(head, count, first)
            if first and head == 1:
                send_part(items - 2)
            if not first and head == group - 1:
                value_grad(items - 1, sent_grad)

        backward(items - 1, edge, sent_grad, beside)
        key_grad(items - 1)
        send_part(items - 1)

    @pl.when(section == sections - 2)
    def _():
        lead = kv_heads - 1
        wait_first()
        wait_second()
        loop(0, kv_heads, lambda item: probabilities(item, 0, group))
        backward(0, edge, sent_grad, nothing)
        for b in range(1, micro):
            wait_later(b)

        def both(item):
            behind = behind_of(item - 1, group // 2)

            def beside(head, count, first):
                behind(head, count, first)
                if not first:
                    probabilities(item + lead, head, count)

            backward(item, edge, sent_grad, beside)
            send_part(item - 1)

        loop(1, items - lead, both)
        loop(items - lead, items - 1, one_sent)
        last_sent()

    @pl.when(section < sections - 2)
    def _():
        wait_first()
        wait_second()
        loop(0, kv_heads, lambda item: probabilities(item, 0, group))
        for b in range(1, micro):
            wait_later(b)
        loop(kv_heads, items, lambda item: probabilities(item, 0, group))
        backward(0, edge, sent_grad, nothing)
        loop(1, items - 1, one_sent)
        last_sent()

    def finish(item):
        @pl.when(has_right)
        def _():
            part_copy(item).wait_recv()

        b, col, _ = place(item)
        for i in range(2):
            total = part_own[item, i] + part_recv[item, i].astype(jnp.float32)
            kv_out[i, b, :, pl.ds(col, DH)] = total.astype(jnp.bfloat16)

    loop(0, items, finish)
    results = tuple(
        pltpu.make_async_copy(kv_out.at[i], ref.at[0], kvg_sem.at[i])
        for i, ref in enumerate((kg_hbm, vg_hbm))
    )
    for copy in results:
        copy.start()

    @pl.when(has_next)
    def _():
        pltpu.make_async_copy(g_out, g_out, g_send).wait()

    @pl.when(has_right)
    def _():
        for b, stage in all_halos:
            for copy in halo_copies(b, stage):
                copy.wait_send()

    @pl.when(has_left)
    def _():
        pltpu.make_async_copy(part_send, part_send, part_send_sem).wait()

    pltpu.make_async_copy(qg_buf, qg_hbm.at[0], qg_sem).wait()
    for copy in results:
        copy.wait()


def hand_over(*refs):
    count = len(refs) // 3
    sources, results, held = refs[:count], refs[count : 2 * count], refs[2 * count : 3 * count]
    sem = refs[3 * count]
    micro = sources[0].shape[1]
    takes, gives = [], []
    for i in range(count):
        for b in range(micro):
            at = (0, b)
            takes.append(pltpu.make_async_copy(sources[i].at[at], held[i].at[at], sem.at[0, i, b]))
            gives.append(pltpu.make_async_copy(held[i].at[at], results[i].at[at], sem.at[1, i, b]))
    for take in takes:
        take.start()
    for take, give in zip(takes, gives):
        take.wait()
        give.start()
    for give in gives:
        give.wait()


def per_device(sections, seq_size, queries, keys, values, out_grad, segments):
    micro, rows, query_width = queries.shape[1:]
    key_width = keys.shape[3]
    kv_heads = key_width // DH
    group = query_width // key_width
    items = micro * kv_heads
    anywhere = pl.BlockSpec(memory_space=pl.ANY)
    low, full = jnp.bfloat16, jnp.float32
    dma = pltpu.SemaphoreType.DMA
    shapes = tuple(jax.ShapeDtypeStruct(x.shape, low) for x in (queries, keys, values))
    grads = pl.pallas_call(
        functools.partial(kernel, sections, seq_size, kv_heads, group),
        out_shape=shapes,
        in_specs=[anywhere] * 5,
        out_specs=(anywhere,) * 3,
        scratch_shapes=[
            pltpu.VMEM((micro, rows, query_width), low),
            pltpu.VMEM((2, micro, 2, rows, key_width), low),
            pltpu.VMEM((micro, rows, query_width), low),
            pltpu.VMEM((items, DH, 2 * rows), low),
            pltpu.VMEM((items, rows, group * DH), full),
            pltpu.VMEM((items, 2 * rows, group * DH), low),
            pltpu.VMEM((items, group, rows, DH), low),
            pltpu.VMEM((items, group, rows, DH), low),
            pltpu.VMEM((micro, rows, query_width), low),
            pltpu.VMEM((items, 2, rows, DH), full),
            pltpu.VMEM((items, 2, rows, DH), low),
            pltpu.VMEM((items, 2, rows, DH), low),
            pltpu.VMEM((2, micro, rows, key_width), low),
            pltpu.VMEM((micro, DH, DH), full),
            pltpu.VMEM((2, DH, DH), low),
            pltpu.VMEM(segments.shape, jnp.int32),
            dma(()),
            dma((micro,)),
            dma((micro,)),
            dma((2, micro)),
            dma((2, micro + 1)),
            dma((2, micro + 1)),
            dma(()),
            dma((items, group)),
            dma(()),
            dma((items,)),
            dma(()),
            dma((2,)),
        ],
        compiler_params=pltpu.CompilerParams(
            collective_id=0, has_side_effects=True, vmem_limit_bytes=60 * 1024 * 1024
        ),
        cost_estimate=pl.CostEstimate(
            flops=10 * items * group * rows * 2 * rows * DH,
            bytes_accessed=6 * 1024 * 1024,
            transcendentals=items * group * rows * rows,
        ),
    )(queries, keys, values, out_grad, segments)
    return pl.pallas_call(
        hand_over,
        out_shape=shapes,
        in_specs=[anywhere] * 3,
        out_specs=(anywhere,) * 3,
        scratch_shapes=[pltpu.VMEM(x.shape, low) for x in shapes] + [dma((2, 3, micro))],
        compiler_params=pltpu.CompilerParams(vmem_limit_bytes=60 * 1024 * 1024),
    )(*grads)


def solution(mesh):
    sizes = dict(mesh.shape)
    split = P("pipe", None, "seq", None)
    return jax.shard_map(
        functools.partial(per_device, sizes["pipe"], sizes["seq"]),
        mesh=mesh,
        in_specs=(split, split, split, P(None, "seq", None), P()),
        out_specs=(split, split, split),
        check_vma=False,
    )
```
